128 devices in a mesh: leaf: 32 (over y, x, core), blk: 4 (over z).
Axes of the slice: x: 4, y: 4, z: 4, core: 2. Of those that a mesh axis runs over, the one named last changes fastest.
Arguments:
- leaf_basis: float32 [2048, 64, 64], P(('leaf', 'blk')), may hold values from -5.5 to 6.5
- leaf_transfer: float32 [2048, 64, 64], P(('leaf', 'blk')), may hold values from -0.5 to 1
- inner_transfer: float32 [2016, 64, 64], P('leaf'), may hold values from -0.5 to 1
- upper_transfer: float32 [31, 64, 64], replicated, may hold values from -0.5 to 1
- coupling: float32 [32768, 64, 64], P(('leaf', 'blk')), may hold values from -6 to 6
- pairs: int32 [32768, 2], P(('leaf', 'blk')), may hold values from 0 to 2047, as said below
- counts: int32 [128], P(('leaf', 'blk')), may hold values from 64 to 256, as said below
Outputs:
- leaf_orth: float32 [2048, 64, 64], P(('leaf', 'blk'))
- new_leaf_transfer: float32 [2048, 64, 64], P(('leaf', 'blk'))
- new_inner_transfer: float32 [2016, 64, 64], P('leaf')
- new_upper: float32 [32, 64, 64], P('leaf')
- reprojected: float32 [32768, 64, 64], P(('leaf', 'blk'))
The draws below stay inside these ranges and needn't reach their ends.
Inputs may be any that keep to these rules, and one draw needn't show every extreme that they name: `pairs`: slots of leaf index d have a row cluster in [d * 64, (d + 1) * 64) and a column cluster in [(d - 1) * 64, (d + 2) * 64). `counts`: the live slots of a device are its leading ones; some device has all 256 live.
All inputs are finite; a program needn't handle non-finite values.
Results may differ from the reference program's by a relative error of at most 0.0003.
Values sent between devices are 32-bit elements; how exact they have to be, the bound alone decides.
A program may use at most 128 MiB of HBM per device.

```python
import math
import jax
import jax.numpy as jnp
from jax import lax

RANK = 64
LEAF = 64
LEAF_DEV = 64
BLK_DEV = 256
LEAVES = 2048
INNER = 2016
UPPER = 31
BLOCKS = 32768
N_LEAF = 32
N_BLK = 4


def transfer_draw(key, number):
    key_two = jax.random.fold_in(key, 1)
    diagonal = jnp.full((number, RANK), 0.6, jnp.float32)
    noise = 0.06 * jnp.clip(jax.random.normal(key_two, (number, RANK, RANK), jnp.float32), -5.0, 5.0)
    return noise + jnp.eye(RANK, dtype=jnp.float32)[None] * diagonal[:, None, :]


def draw_leaf_basis(key, part):
    key_one = jax.random.fold_in(key, 0)
    key_two = jax.random.fold_in(key, 1)
    key_four = jax.random.fold_in(key, 3)
    key_five = jax.random.fold_in(key, 4)
    ratio = jax.random.uniform(key_four, (LEAVES, RANK), jnp.float32, 0.6, 0.85)
    signs = jnp.where(jax.random.bernoulli(key_five, 0.5, (LEAVES, RANK)), jnp.float32(1.0), jnp.float32(-1.0))
    diagonal = jnp.exp(jax.random.uniform(key_one, (LEAVES, RANK), jnp.float32, 0.0, math.log(3.0)))
    noise = 0.02 * jnp.clip(jax.random.normal(key_two, (LEAVES, LEAF, RANK), jnp.float32), -5.0, 5.0)
    upper_band = signs * ratio * diagonal
    main_part = jnp.eye(LEAF, RANK, dtype=jnp.float32)[None] * diagonal[:, None, :]
    band_part = jnp.eye(LEAF, RANK, k=1, dtype=jnp.float32)[None] * upper_band[:, None, :]
    return noise + main_part + band_part


def draw_leaf_transfer(key, part):
    return transfer_draw(jax.random.fold_in(key, 11), LEAVES)


def draw_inner_transfer(key, part):
    return transfer_draw(jax.random.fold_in(key, 12), INNER)


def draw_upper_transfer(key, part):
    return transfer_draw(jax.random.fold_in(key, 13), UPPER)


def draw_pairs(key, part):
    key_one, key_two = jax.random.split(jax.random.fold_in(key, 21), 2)
    slots = jnp.arange(BLOCKS, dtype=jnp.int32)
    subtree = slots // (BLK_DEV * N_BLK)
    row_pick = subtree * LEAF_DEV + jax.random.randint(key_one, (BLOCKS,), 0, LEAF_DEV, dtype=jnp.int32)
    lowest = jnp.maximum(subtree - 1, 0) * LEAF_DEV
    highest_end = jnp.minimum(subtree + 2, N_LEAF) * LEAF_DEV
    col_pick = jax.random.randint(key_two, (BLOCKS,), lowest, highest_end, dtype=jnp.int32)
    return jnp.stack([row_pick, col_pick], axis=1)


def draw_counts(key, part):
    key_one, key_two = jax.random.split(jax.random.fold_in(key, 31), 2)
    total = N_LEAF * N_BLK
    drawn = jax.random.randint(key_one, (total,), BLK_DEV // 4, BLK_DEV + 1, dtype=jnp.int32)
    fullest = jax.random.randint(key_two, (), 0, total, dtype=jnp.int32)
    return jnp.where(jnp.arange(total, dtype=jnp.int32) == fullest, jnp.int32(BLK_DEV), drawn)


def block_scale(own_key, dims, cuts, low, largest):
    def one(dim, parts):
        heights = jax.random.uniform(jax.random.fold_in(jax.random.fold_in(own_key, 6), dim), (parts,), jnp.float32, low / len(cuts), largest / len(cuts))
        return jnp.repeat(jnp.exp(heights), dims[dim] // parts).reshape((-1,) + (1,) * (len(dims) - dim - 1))

    loudness = one(*cuts[0])
    for cut in cuts[1:]:
        loudness = loudness * one(*cut)
    return loudness


def gaussian(own_key, dims, deviation, bound, pieces=(), kind=jnp.bfloat16):
    values = jax.random.normal(own_key, dims, jnp.float32) * deviation
    if len(pieces) > 0:
        values = block_scale(own_key, dims, pieces, -0.22, 0.18) * values
    return jnp.clip(values, min=-bound, max=bound).astype(kind)


def setup_inputs(seed: int = 0) -> dict:
    arg_keys = jax.random.split(jax.random.key(seed), 8)
    return {
        "leaf_basis": draw_leaf_basis(jax.random.fold_in(arg_keys[7], 71), 0),
        "leaf_transfer": draw_leaf_transfer(jax.random.fold_in(arg_keys[7], 71), 0),
        "inner_transfer": draw_inner_transfer(jax.random.fold_in(arg_keys[7], 71), 0),
        "upper_transfer": draw_upper_transfer(jax.random.fold_in(arg_keys[7], 71), 0),
        "coupling": gaussian(arg_keys[4], (BLOCKS, RANK, RANK), 1.0, 6.0, ((0, 128),), jnp.float32),
        "pairs": draw_pairs(jax.random.fold_in(arg_keys[7], 71), 0),
        "counts": draw_counts(jax.random.fold_in(arg_keys[7], 71), 0),
    }


highest = lax.Precision.HIGHEST

def times_right(left, right):
    return jnp.einsum('...ab,...bc->...ac', left, right, precision=highest)

def transpose_times(left, right):
    return jnp.einsum('...ba,...bc->...ac', left, right, precision=highest)

def flipped(matrix):
    return jnp.swapaxes(matrix, -1, -2)

def sandwich(transfer, gram):
    return transpose_times(transfer, times_right(gram, transfer))

def retransfer(child_factor, transfer, parent_factor):
    carried = transpose_times(child_factor, transfer)
    solved = lax.linalg.triangular_solve(parent_factor, flipped(carried), left_side=True, lower=True)
    return flipped(solved)

def reference(leaf_basis, leaf_transfer, inner_transfer, upper_transfer, coupling, pairs, counts):
    group = LEAF_DEV
    nleaf = N_LEAF
    leaf_gram = transpose_times(leaf_basis, leaf_basis)
    factor = jnp.linalg.cholesky(leaf_gram)
    leaf_orth = flipped(lax.linalg.triangular_solve(factor, flipped(leaf_basis), left_side=True, lower=True))
    images = sandwich(leaf_transfer, leaf_gram).reshape(nleaf, group, RANK, RANK)
    child_factor = factor.reshape(nleaf, group, RANK, RANK)
    child_transfer = leaf_transfer.reshape(nleaf, group, RANK, RANK)
    inner_all = inner_transfer.reshape(nleaf, group - 1, RANK, RANK)
    levels = group.bit_length() - 1
    new_leaf = None
    inner_parts = []
    for level in range(levels - 1, -1, -1):
        node_gram = images[:, 0::2] + images[:, 1::2]
        node_factor = jnp.linalg.cholesky(node_gram)
        renewed = retransfer(child_factor, child_transfer, jnp.repeat(node_factor, 2, axis=1))
        if new_leaf is None:
            new_leaf = renewed.reshape(LEAVES, RANK, RANK)
        else:
            inner_parts.insert(0, renewed)
        node_transfer = inner_all[:, 2 ** level - 1:2 ** (level + 1) - 1]
        images = sandwich(node_transfer, node_gram)
        child_factor = node_factor
        child_transfer = node_transfer
    upper_images = images[:, 0]
    prev_factor = child_factor[:, 0]
    prev_transfer = child_transfer[:, 0]
    upward = nleaf.bit_length() - 1
    new_upper = jnp.zeros((nleaf, RANK, RANK), jnp.float32)
    root_renewed = None
    for level in range(1, upward + 1):
        node_gram = upper_images[0::2] + upper_images[1::2]
        node_factor = jnp.linalg.cholesky(node_gram)
        renewed = retransfer(prev_factor, prev_transfer, jnp.repeat(node_factor, 2, axis=0))
        if level == 1:
            root_renewed = renewed
        else:
            new_upper = new_upper.at[2 ** (level - 2)::2 ** (level - 1)].set(renewed)
        node_transfer = upper_transfer[2 ** (level - 1) - 1::2 ** level]
        upper_images = sandwich(node_transfer, node_gram)
        prev_factor = node_factor
        prev_transfer = node_transfer
    new_upper = new_upper.at[2 ** (upward - 1)].set(transpose_times(prev_factor, prev_transfer)[0])
    new_upper = new_upper.at[0].set(flipped(prev_factor[0]))
    new_inner = jnp.concatenate([root_renewed[:, None]] + inner_parts, axis=1).reshape(INNER, RANK, RANK)
    devices = N_LEAF * N_BLK
    blocks = coupling.reshape(devices, BLK_DEV, RANK, RANK)
    slot_pairs = pairs.reshape(devices, BLK_DEV, 2)

    def project(packed):
        block_set, pair_set, live_count = packed
        row_factor = factor[pair_set[:, 0]]
        col_factor = factor[pair_set[:, 1]]
        result = transpose_times(row_factor, times_right(block_set, col_factor))
        live = jnp.arange(BLK_DEV, dtype=jnp.int32) < live_count
        return jnp.where(live[:, None, None], result, jnp.float32(0.0))
    reprojected = lax.map(project, (blocks, slot_pairs, counts)).reshape(BLOCKS, RANK, RANK)
    return (leaf_orth, new_leaf, new_inner, new_upper, reprojected)
```

```python
import jax
import jax.numpy as jnp
from jax import lax
from jax.experimental import pallas as pl
from jax.experimental.pallas import tpu as pltpu
from jax.sharding import PartitionSpec as P

HIGH = lax.Precision.HIGHEST
F32 = jnp.float32
N = 64


def nn(a, b):
    return lax.dot_general(a, b, (((1,), (0,)), ((), ())), precision=HIGH, preferred_element_type=F32)


def tn(a, b):
    return lax.dot_general(a, b, (((0,), (0,)), ((), ())), precision=HIGH, preferred_element_type=F32)


def nt(a, b):
    return lax.dot_general(a, b, (((1,), (1,)), ((), ())), precision=HIGH, preferred_element_type=F32)


def sandwich(e, g):
    return tn(e, nn(g, e))


def local_tree(pos_ref, basis_ref, lt_ref, it_ref, gram_ref, img_ref, tmp):
    blk = pos_ref[1]
    for c in range(16):
        b = basis_ref[c]
        g = tn(b, b)
        gram_ref[c] = g
        tmp[c] = sandwich(lt_ref[c], g)
    at, src = 16, 0
    for count in (8, 4, 2, 1):
        for n in range(count):
            g = tmp[src + 2 * n] + tmp[src + 2 * n + 1]
            gram_ref[at + n] = g
            m = sandwich(it_ref[4 * count - 1 + count * blk + n], g)
            if count == 1:
                img_ref[...] = m
                gram_ref[31] = g
            else:
                tmp[src + 2 * count + n] = m
        src += 2 * count
        at += count


def run_local_tree(pos, basis, lt, it):
    vm = pl.BlockSpec(memory_space=pltpu.VMEM)
    return pl.pallas_call(
        local_tree,
        out_shape=(jax.ShapeDtypeStruct((32, N, N), F32), jax.ShapeDtypeStruct((N, N), F32)),
        in_specs=[pl.BlockSpec(memory_space=pltpu.SMEM), vm, vm, vm],
        out_specs=(vm, vm),
        scratch_shapes=[pltpu.VMEM((32, N, N), F32)],
        compiler_params=pltpu.CompilerParams(vmem_limit_bytes=40 * 2**20),
    )(pos, basis, lt, it)


def eliminate(a_ref, w_ref, lanes):
    sub = lax.broadcasted_iota(jnp.int32, (8, lanes), 0)

    def bc(x, i):
        return jnp.broadcast_to(x[i:i + 1, :], (8, lanes))

    for p in range(8):
        k0 = 8 * p
        d = [a_ref[k0 + i, k0:k0 + 8, :] for i in range(8)]
        r = []
        coef = {}
        for k in range(8):
            piv = bc(d[k], k)
            y = lax.rsqrt(piv)
            y = y * (1.5 - 0.5 * piv * y * y)
            r.append(y)
            d[k] = d[k] * y
            for i in range(k + 1, 8):
                coef[k, i] = bc(d[k], i)
                d[i] = d[i] - coef[k, i] * d[k]
        for i in range(8):
            a_ref[k0 + i, k0:k0 + 8, :] = d[i]

        def solve(x):
            for k in range(8):
                x[k] = x[k] * r[k]
                for i in range(k + 1, 8):
                    x[i] = x[i] - coef[k, i] * x[k]
            return x

        for jb in range(p + 1, 8):
            x = solve([a_ref[k0 + i, 8 * jb:8 * jb + 8, :] for i in range(8)])
            for i in range(8):
                a_ref[k0 + i, 8 * jb:8 * jb + 8, :] = x[i]
        for jb in range(p + 1):
            if jb < p:
                x = [w_ref[k0 + i, 8 * jb:8 * jb + 8, :] for i in range(8)]
            else:
                x = [jnp.where(sub == i, F32(1), F32(0)) for i in range(8)]
            x = solve(x)
            for i in range(8):
                w_ref[k0 + i, 8 * jb:8 * jb + 8, :] = x[i]

        for ib in range(p + 1, 8):
            def step(t, _, ib=ib, p=p, k0=k0):
                i = 8 * ib + t
                cs = [jnp.broadcast_to(a_ref[k0 + k, pl.ds(i, 1), :], (8, lanes)) for k in range(8)]
                for jb in range(ib, 8):
                    acc = a_ref[i, 8 * jb:8 * jb + 8, :]
                    for k in range(8):
                        acc = acc - cs[k] * a_ref[k0 + k, 8 * jb:8 * jb + 8, :]
                    a_ref[i, 8 * jb:8 * jb + 8, :] = acc
                for jb in range(p + 1):
                    acc = w_ref[i, 8 * jb:8 * jb + 8, :] if jb < p else jnp.zeros((8, lanes), F32)
                    for k in range(8):
                        acc = acc - cs[k] * w_ref[k0 + k, 8 * jb:8 * jb + 8, :]
                    w_ref[i, 8 * jb:8 * jb + 8, :] = acc
                return 0
            lax.fori_loop(0, 8, step, 0)


def chain(m_ref, it_ref, up_ref, g_ref, quad, octet, four, send_sem, recv_sem):
    leaf, blk = lax.axis_index("leaf"), lax.axis_index("blk")
    low, high = leaf % 8, leaf // 8
    near = [({"leaf": leaf, "blk": (blk + i) % 4}) for i in range(1, 4)]
    mid = [({"leaf": high * 8 + (low + i) % 8, "blk": blk}) for i in range(1, 8)]
    far = [({"leaf": ((high + i) % 4) * 8 + low, "blk": blk}) for i in range(1, 4)]
    peers = near + mid + far
    barrier = pltpu.get_barrier_semaphore()
    for peer in peers:
        pl.semaphore_signal(barrier, inc=1, device_id=peer, device_id_type=pl.DeviceIdType.MESH)
    pl.semaphore_wait(barrier, len(peers))

    def exchange(value, slots, place, group, base):
        slots[place] = value
        copies = []
        for t, peer in enumerate(group):
            c = pltpu.make_async_remote_copy(
                src_ref=slots.at[place], dst_ref=slots.at[place],
                send_sem=send_sem.at[base + t], recv_sem=recv_sem.at[base + t],
                device_id=peer, device_id_type=pl.DeviceIdType.MESH)
            c.start()
            copies.append(c)
        for c in copies:
            c.wait()

    exchange(m_ref[...], quad, blk, near, 0)
    root = None
    for n in range(2):
        g = quad[2 * n] + quad[2 * n + 1]
        g_ref[n] = g
        m = sandwich(it_ref[1 + n], g)
        root = m if root is None else root + m
    g_ref[2] = root
    exchange(sandwich(it_ref[0], root), octet, low, mid, 3)
    first = [octet[2 * n] + octet[2 * n + 1] for n in range(4)]
    g_ref[3] = octet[low // 2 * 2] + octet[low // 2 * 2 + 1]
    images = [sandwich(up_ref[high * 8 + 2 * n], first[n]) for n in range(4)]
    second = [images[2 * n] + images[2 * n + 1] for n in range(2)]
    g_ref[4] = jnp.where(low < 4, second[0], second[1])
    images = [sandwich(up_ref[high * 8 + 4 * n + 1], second[n]) for n in range(2)]
    third = images[0] + images[1]
    g_ref[5] = third
    exchange(sandwich(up_ref[high * 8 + 3], third), four, high, far, 10)
    fourth = [four[2 * n] + four[2 * n + 1] for n in range(2)]
    g_ref[6] = jnp.where(high < 2, fourth[0], fourth[1])
    images = [sandwich(up_ref[16 * n + 7], fourth[n]) for n in range(2)]
    g_ref[7] = images[0] + images[1]


def run_chain(m, it, up):
    vm = pl.BlockSpec(memory_space=pltpu.VMEM)
    return pl.pallas_call(
        chain,
        out_shape=jax.ShapeDtypeStruct((8, N, N), F32),
        in_specs=[vm, vm, vm],
        out_specs=vm,
        scratch_shapes=[
            pltpu.VMEM((4, N, N), F32), pltpu.VMEM((8, N, N), F32), pltpu.VMEM((4, N, N), F32),
            pltpu.SemaphoreType.DMA((13,)), pltpu.SemaphoreType.DMA((13,)),
        ],
        compiler_params=pltpu.CompilerParams(collective_id=0, has_side_effects=True, vmem_limit_bytes=40 * 2**20),
    )(m, it, up)


def factors(pos_ref, g1_ref, g2_ref, basis_ref, lt_ref, it_ref, up_ref,
            orth_ref, newleaf_ref, pack_ref, shared_ref, upper_ref, upack_ref, a, w, u):
    leaf, blk = pos_ref[0], pos_ref[1]

    def load(k, _):
        x = jnp.concatenate([g1_ref[pl.ds(k, 32, stride=N), :], g2_ref[pl.ds(k, 8, stride=N), :]], axis=0)
        a[k] = x.T
        return 0
    lax.fori_loop(0, N, load, 0, unroll=4)
    eliminate(a, w, 40)
    col = lax.broadcasted_iota(jnp.int32, (N, 40), 0)

    def save(k, _):
        u[0, pl.ds(k, 40, stride=N), :] = jnp.where(col >= k, a[k], F32(0)).T
        u[1, pl.ds(k, 40, stride=N), :] = jnp.where(col <= k, w[k], F32(0)).T
        return 0
    lax.fori_loop(0, N, save, 0, unroll=4)

    def up(i):
        return u[0, pl.ds(i * N, N), :]

    def inverse(i):
        return u[1, pl.ds(i * N, N), :]

    for c in range(8):
        upack_ref[c] = jnp.concatenate([up(2 * c), up(2 * c + 1)], axis=1)
    for c in range(16):
        orth_ref[c] = nt(basis_ref[c], inverse(c))
        newleaf_ref[c] = nt(nn(up(c), lt_ref[c]), inverse(16 + c // 2))
    done = []
    at = 16
    for count in (8, 4, 2, 1):
        for n in range(count):
            e = it_ref[4 * count - 1 + count * blk + n]
            parent = at + count + n // 2 if count > 1 else 32 + blk // 2
            done.append(nt(nn(up(at + n), e), inverse(parent)))
        at += count
    done.append(done[-1])
    for c in range(8):
        pack_ref[c] = jnp.concatenate([done[2 * c], done[2 * c + 1]], axis=1)
    shared_ref[0] = nt(nn(up(34), it_ref[0]), inverse(35))
    for n in range(2):
        shared_ref[1 + n] = nt(nn(up(32 + n), it_ref[1 + n]), inverse(34))
    level = jnp.where(leaf % 2 == 1, 1, jnp.where(leaf % 4 == 2, 2, jnp.where(leaf % 8 == 4, 3, jnp.where(leaf % 16 == 8, 4, 5))))
    carried = nn(up(34 + level), up_ref[jnp.maximum(leaf - 1, 0)])
    renewed = nt(carried, inverse(jnp.minimum(35 + level, 39)))
    upper_ref[0] = jnp.where(leaf == 0, up(39), jnp.where(leaf == 16, carried, renewed))


def run_factors(pos, g1, g2, basis, lt, it, up):
    vm = pl.BlockSpec(memory_space=pltpu.VMEM)
    sd = jax.ShapeDtypeStruct
    return pl.pallas_call(
        factors,
        out_shape=(sd((16, N, N), F32), sd((16, N, N), F32), sd((8, N, 2 * N), F32), sd((3, N, N), F32),
                   sd((1, N, N), F32), sd((8, N, 2 * N), F32)),
        in_specs=[pl.BlockSpec(memory_space=pltpu.SMEM)] + [vm] * 6,
        out_specs=(vm,) * 6,
        scratch_shapes=[pltpu.VMEM((N, N, 40), F32), pltpu.VMEM((N, N, 40), F32), pltpu.VMEM((2, 40 * N, N), F32)],
        compiler_params=pltpu.CompilerParams(vmem_limit_bytes=48 * 2**20),
    )(pos, g1.reshape(32 * N, N), g2.reshape(8 * N, N), basis, lt, it, up)


def spread(u_ref, t_ref, all_u, all_t, send_sem, recv_sem, local_sem):
    leaf, blk = lax.axis_index("leaf"), lax.axis_index("blk")
    near = [{"leaf": leaf, "blk": (blk + i) % 4} for i in range(1, 4)]
    right = {"leaf": (leaf + 1) % 32, "blk": blk}
    left = {"leaf": (leaf + 31) % 32, "blk": blk}
    barrier = pltpu.get_barrier_semaphore()
    for peer in near + [right, left]:
        pl.semaphore_signal(barrier, inc=1, device_id=peer, device_id_type=pl.DeviceIdType.MESH)
    pl.semaphore_wait(barrier, 5)

    def push(src, dst, sem, peer):
        c = pltpu.make_async_remote_copy(
            src_ref=src, dst_ref=dst, send_sem=send_sem.at[sem], recv_sem=recv_sem.at[sem],
            device_id=peer, device_id_type=pl.DeviceIdType.MESH)
        c.start()
        return c

    own_u = pltpu.make_async_copy(u_ref, all_u.at[1, blk], local_sem.at[0])
    own_t = pltpu.make_async_copy(t_ref, all_t.at[blk], local_sem.at[1])
    own_u.start()
    own_t.start()
    hops = [push(u_ref, all_u.at[1, blk], i, near[i]) for i in (0, 2, 1)]
    rest = [push(u_ref, all_u.at[0, blk], 3, right), push(u_ref, all_u.at[2, blk], 4, left)]
    rest += [push(t_ref, all_t.at[blk], 5 + i, near[i]) for i in (0, 2, 1)]
    for c, i in zip(hops, (1, 3, 2)):
        c.wait_recv()
        got = (blk + 4 - i) % 4
        rest.append(push(all_u.at[1, got], all_u.at[0, got], 8 + 2 * (i - 1), right))
        rest.append(push(all_u.at[1, got], all_u.at[2, got], 9 + 2 * (i - 1), left))
    own_u.wait()
    own_t.wait()
    for c in hops:
        c.wait_send()
    for c in rest:
        c.wait()


def run_spread(u, t):
    vm = pl.BlockSpec(memory_space=pltpu.VMEM)
    sd = jax.ShapeDtypeStruct
    return pl.pallas_call(
        spread,
        out_shape=(sd((3, 4, 8, N, 2 * N), F32), sd((4, 8, N, 2 * N), F32)),
        in_specs=[vm, vm],
        out_specs=(vm, vm),
        scratch_shapes=[pltpu.SemaphoreType.DMA((14,)), pltpu.SemaphoreType.DMA((14,)), pltpu.SemaphoreType.DMA((2,))],
        compiler_params=pltpu.CompilerParams(collective_id=1, has_side_effects=True, vmem_limit_bytes=40 * 2**20),
    )(u, t)


BF = jnp.bfloat16


def split(x):
    h = x.astype(BF).astype(F32)
    return h, (x - h).astype(BF).astype(F32)


def project(pair_ref, count_ref, c_ref, u_ref, t_ref, shared_ref, out_ref, inner_ref, s, cols, rows):
    lane = lax.broadcasted_iota(jnp.int32, (N, 2 * N), 1)
    first = lane < N

    def turn(a, _):
        x = jnp.concatenate([c_ref[a, :, 0:128], c_ref[a, :, 128:256]], axis=0)
        s[pl.ds(a, 128, stride=N), :] = x.T
        return 0
    lax.fori_loop(0, N, turn, 0, unroll=2)

    def cut(x):
        h, l = split(x)
        return h, l, pltpu.roll(h, N, 1), pltpu.roll(l, N, 1)

    def prepare(p, _):
        h, l, hr, lr = cut(u_ref[p])
        cols[2 * p] = jnp.concatenate([jnp.where(first, h, hr), jnp.where(first, l, lr)], axis=1).astype(BF)
        cols[2 * p + 1] = jnp.concatenate([jnp.where(first, hr, h), jnp.where(first, lr, l)], axis=1).astype(BF)
        return 0
    lax.fori_loop(0, 96, prepare, 0, unroll=2)

    def prepare_rows(p, _):
        h, l, hr, lr = cut(u_ref[32 + p])
        rows[2 * p] = jnp.where(first, h, lr).astype(BF)
        rows[2 * p + 1] = jnp.where(first, hr, l).astype(BF)
        return 0
    lax.fori_loop(0, 32, prepare_rows, 0, unroll=2)

    base = pair_ref[2, 0]

    def slot(k, d):
        i = jnp.clip(pair_ref[0, k] - base, 0, 63)
        j = jnp.clip(pair_ref[1, k] - base + 64, 0, 191)
        d = d.astype(BF)
        y = lax.dot_general(jnp.concatenate([d, d], axis=1), cols[j], (((1,), (1,)), ((), ())), preferred_element_type=F32)
        h = y.astype(BF)
        l = (y - h.astype(F32)).astype(BF)
        r = rows[i]
        return lax.dot_general(jnp.concatenate([r, r], axis=1), jnp.concatenate([h, h, l, l], axis=0),
                               (((1,), (0,)), ((), ())), preferred_element_type=F32)

    def both(k, _):
        at = pl.ds(pl.multiple_of(k * N, N), N)
        h, l, hr, lr = cut(s[at, :])
        s[at, :] = jnp.concatenate([slot(k, jnp.where(first, h, lr)), slot(k + 128, jnp.where(first, hr, l))], axis=1)
        return 0
    lax.fori_loop(0, 128, both, 0, unroll=4)

    def back(a, _):
        x = s[pl.ds(a, 128, stride=N), :].T
        out_ref[a, :, 0:128] = jnp.where(lane < count_ref[0], x[:N], F32(0))
        out_ref[a, :, 128:256] = jnp.where(lane + 128 < count_ref[0], x[N:], F32(0))
        return 0
    lax.fori_loop(0, N, back, 0, unroll=2)

    for n in range(3):
        inner_ref[n] = shared_ref[n]
    for b in range(4):
        at = 0
        for count in (8, 4, 2, 1):
            for n in range(count):
                inner_ref[4 * count - 1 + count * b + n] = t_ref[b, at // 2, :, (at % 2) * N:(at % 2) * N + N]
                at += 1


def run_project(pairs, counts, base, coupling, u, t, shared):
    vm = pl.BlockSpec(memory_space=pltpu.VMEM)
    sm = pl.BlockSpec(memory_space=pltpu.SMEM)
    sd = jax.ShapeDtypeStruct
    table = jnp.concatenate([pairs.T, jnp.broadcast_to(base, (1, 256))], axis=0)
    out, inner = pl.pallas_call(
        project,
        out_shape=(sd((N, N, 256), F32), sd((63, N, N), F32)),
        in_specs=[sm, sm, vm, vm, vm, vm],
        out_specs=(vm, vm),
        scratch_shapes=[pltpu.VMEM((128 * N, 2 * N), F32), pltpu.VMEM((192, N, 4 * N), BF), pltpu.VMEM((64, N, 2 * N), BF)],
        compiler_params=pltpu.CompilerParams(vmem_limit_bytes=60 * 2**20),
    )(table, counts, jnp.transpose(coupling, (1, 2, 0)), u.reshape(96, N, 2 * N), t, shared)
    return jnp.transpose(out, (2, 0, 1)), inner


def body(leaf_basis, leaf_transfer, inner_transfer, upper_transfer, coupling, pairs, counts):
    leaf, blk = lax.axis_index("leaf"), lax.axis_index("blk")
    pos = jnp.stack([leaf, blk]).astype(jnp.int32)
    g1, m = run_local_tree(pos, leaf_basis, leaf_transfer, inner_transfer)
    g2 = run_chain(m, inner_transfer, upper_transfer)
    orth, new_leaf, pack, shared, upper, upack = run_factors(
        pos, g1, g2, leaf_basis, leaf_transfer, inner_transfer, upper_transfer)
    all_u, all_t = run_spread(upack, pack)
    out, inner = run_project(pairs, counts, (leaf * 64).astype(jnp.int32), coupling, all_u, all_t, shared)
    return orth, new_leaf, inner, upper, out


def solution(mesh):
    in_specs = (
        P(("leaf", "blk"), None, None),
        P(("leaf", "blk"), None, None),
        P("leaf", None, None),
        P(),
        P(("leaf", "blk"), None, None),
        P(("leaf", "blk"), None),
        P(("leaf", "blk")),
    )
    out_specs = (
        P(("leaf", "blk"), None, None),
        P(("leaf", "blk"), None, None),
        P("leaf", None, None),
        P("leaf", None, None),
        P(("leaf", "blk"), None, None),
    )
    return jax.shard_map(body, mesh=mesh, in_specs=in_specs, out_specs=out_specs, check_vma=False)
```

```python
import jax
import jax.numpy as jnp
from jax import lax
from jax.experimental import pallas as pl
from jax.experimental.pallas import tpu as pltpu
from jax.sharding import PartitionSpec as P

HIGH = lax.Precision.HIGHEST
F32 = jnp.float32
N = 64


def nn(a, b):
    return lax.dot_general(a, b, (((1,), (0,)), ((), ())), precision=HIGH, preferred_element_type=F32)


def tn(a, b):
    return lax.dot_general(a, b, (((0,), (0,)), ((), ())), precision=HIGH, preferred_element_type=F32)


def nt(a, b):
    return lax.dot_general(a, b, (((1,), (1,)), ((), ())), precision=HIGH, preferred_element_type=F32)


def sandwich(e, g):
    return tn(e, nn(g, e))


def local_tree(pos_ref, basis_ref, lt_ref, it_ref, gram_ref, img_ref, tmp):
    blk = pos_ref[1]
    for c in range(16):
        b = basis_ref[c]
        g = tn(b, b)
        gram_ref[c] = g
        tmp[c] = sandwich(lt_ref[c], g)
    at, src = 16, 0
    for count in (8, 4, 2, 1):
        for n in range(count):
            g = tmp[src + 2 * n] + tmp[src + 2 * n + 1]
            gram_ref[at + n] = g
            m = sandwich(it_ref[4 * count - 1 + count * blk + n], g)
            if count == 1:
                img_ref[...] = jnp.concatenate([g, m], axis=1)
                gram_ref[31] = g
            else:
                tmp[src + 2 * count + n] = m
        src += 2 * count
        at += count


def run_local_tree(pos, basis, lt, it):
    vm = pl.BlockSpec(memory_space=pltpu.VMEM)
    return pl.pallas_call(
        local_tree,
        out_shape=(jax.ShapeDtypeStruct((32, N, N), F32), jax.ShapeDtypeStruct((N, 2 * N), F32)),
        in_specs=[pl.BlockSpec(memory_space=pltpu.SMEM), vm, vm, vm],
        out_specs=(vm, vm),
        scratch_shapes=[pltpu.VMEM((32, N, N), F32)],
        compiler_params=pltpu.CompilerParams(vmem_limit_bytes=40 * 2**20),
    )(pos, basis, lt, it)


LANES = 128
COPIES = 29


def eliminate(a_ref, w_ref):
    sub = lax.broadcasted_iota(jnp.int32, (8, LANES), 0)

    def bc(x, i):
        return jnp.broadcast_to(x[i:i + 1, :], (8, LANES))

    def panel(p):
        k0 = 8 * p
        d = [a_ref[k0 + i, k0:k0 + 8, :] for i in range(8)]
        r, coef = [], {}
        for k in range(8):
            piv = bc(d[k], k)
            y = lax.rsqrt(piv)
            y = y * (1.5 - 0.5 * piv * y * y)
            r.append(y)
            d[k] = d[k] * y
            for i in range(k + 1, 8):
                coef[k, i] = bc(d[k], i)
                d[i] = d[i] - coef[k, i] * d[k]
        for i in range(8):
            a_ref[k0 + i, k0:k0 + 8, :] = d[i]

        def solve(x):
            for k in range(8):
                x[k] = x[k] * r[k]
                for i in range(k + 1, 8):
                    x[i] = x[i] - coef[k, i] * x[k]
            return x

        for jb in range(p + 1, 8):
            x = solve([a_ref[k0 + i, 8 * jb:8 * jb + 8, :] for i in range(8)])
            for i in range(8):
                a_ref[k0 + i, 8 * jb:8 * jb + 8, :] = x[i]
        for jb in range(p + 1):
            if jb < p:
                x = [w_ref[k0 + i, 8 * jb:8 * jb + 8, :] for i in range(8)]
            else:
                x = [jnp.where(sub == i, F32(1), F32(0)) for i in range(8)]
            x = solve(x)
            for i in range(8):
                w_ref[k0 + i, 8 * jb:8 * jb + 8, :] = x[i]

    def trail(p, row, targets):
        k0 = 8 * p
        for g in range(0, len(targets), 2):
            group = targets[g:g + 2]
            acc = {}
            for t, (ref, jb, fresh) in enumerate(group):
                for i in range(8):
                    acc[t, i] = jnp.zeros((8, LANES), F32) if fresh else ref[row + i, 8 * jb:8 * jb + 8, :]
            for k in range(8):
                pivots = [ref[k0 + k, 8 * jb:8 * jb + 8, :] for ref, jb, _ in group]
                for i in range(8):
                    c = jnp.broadcast_to(a_ref[k0 + k, pl.ds(row + i, 1), :], (8, LANES))
                    for t in range(len(group)):
                        acc[t, i] = acc[t, i] - c * pivots[t]
            for t, (ref, jb, _) in enumerate(group):
                for i in range(8):
                    ref[row + i, 8 * jb:8 * jb + 8, :] = acc[t, i]

    for p in range(8):
        panel(p)
        targets = [(a_ref, jb, False) for jb in range(p + 1, 8)] + [(w_ref, jb, jb == p) for jb in range(p + 1)]

        def step(ib, _):
            trail(p, 8 * ib, targets)
            return 0
        lax.fori_loop(p + 1, 8, step, 0)


def factor_stack(g_ref, u_ref, w_ref, a, w, n):
    def load(k, _):
        a[k, :, 0:n] = g_ref[pl.ds(k, n, stride=N), :].T
        return 0
    lax.fori_loop(0, N, load, 0, unroll=8)
    eliminate(a, w)
    col = lax.broadcasted_iota(jnp.int32, (N, n), 0)

    def save(k, _):
        u_ref[pl.ds(k, n, stride=N), :] = jnp.where(col >= k, a[k, :, 0:n], F32(0)).T
        w_ref[pl.ds(k, n, stride=N), :] = jnp.where(col <= k, w[k, :, 0:n], F32(0)).T
        return 0
    lax.fori_loop(0, N, save, 0, unroll=8)


def lower_factors(g_ref, u_ref, w_ref, pack_ref, a, w):
    factor_stack(g_ref, u_ref, w_ref, a, w, 32)
    for c in range(8):
        pack_ref[c] = jnp.concatenate([u_ref[2 * c * N:2 * c * N + N, :], u_ref[2 * c * N + N:2 * c * N + 2 * N, :]], axis=1)


def run_lower_factors(g):
    vm = pl.BlockSpec(memory_space=pltpu.VMEM)
    s = jax.ShapeDtypeStruct((32 * N, N), F32)
    return pl.pallas_call(
        lower_factors,
        out_shape=(s, s, jax.ShapeDtypeStruct((8, N, 2 * N), F32)),
        in_specs=[vm],
        out_specs=(vm, vm, vm),
        scratch_shapes=[pltpu.VMEM((N, N, LANES), F32)] * 2,
        compiler_params=pltpu.CompilerParams(vmem_limit_bytes=40 * 2**20),
    )(g.reshape(32 * N, N))


BF = jnp.bfloat16


def split(x):
    h = x.astype(BF).astype(F32)
    return h, (x - h).astype(BF).astype(F32)


def cut(x):
    h, l = split(x)
    return h, l, pltpu.roll(h, N, 1), pltpu.roll(l, N, 1)


def middle(table_ref, count_ref, gm_ref, pack_ref, u_ref, w_ref, basis_ref, lt_ref, it_ref, up_ref, c_ref,
           orth_ref, newleaf_ref, g_ref, inner_ref, out_ref,
           buf, s, r, cols, rows, all_u, all_t, quad, octet, four, send_sem, recv_sem, local_sem):
    leaf, blk = lax.axis_index("leaf"), lax.axis_index("blk")
    low, high = leaf % 8, leaf // 8
    zup, zdown, zfar = [{"leaf": leaf, "blk": (blk + i) % 4} for i in (1, 3, 2)]
    right = {"leaf": (leaf + 1) % 32, "blk": blk}
    left = {"leaf": (leaf + 31) % 32, "blk": blk}
    mid = [{"leaf": high * 8 + (low + i) % 8, "blk": blk} for i in range(1, 8)]
    far = [{"leaf": (high + i) % 4 * 8 + low, "blk": blk} for i in range(1, 4)]
    peers = [zup, zdown, zfar, right, left] + mid + far
    barrier = pltpu.get_barrier_semaphore()
    for peer in peers:
        pl.semaphore_signal(barrier, inc=1, device_id=peer, device_id_type=pl.DeviceIdType.MESH)
    fetch = pltpu.make_async_copy(c_ref, buf, local_sem.at[0])
    fetch.start()
    own_u = pltpu.make_async_copy(pack_ref, all_u.at[pl.ds((4 + blk) * 8, 8)], local_sem.at[1])
    own_u.start()
    used = []

    def push(src, dst, peer):
        i = len(used)
        c = pltpu.make_async_remote_copy(
            src_ref=src, dst_ref=dst, send_sem=send_sem.at[i], recv_sem=recv_sem.at[i],
            device_id=peer, device_id_type=pl.DeviceIdType.MESH)
        c.start()
        used.append(c)
        return c

    def block(d, b, start, count):
        return all_u.at[pl.ds((d * 4 + b) * 8 + start, count)]

    def u(i):
        return u_ref[i * N:i * N + N, :]

    def w(i):
        return w_ref[i * N:i * N + N, :]

    def orth(c):
        orth_ref[c] = nt(basis_ref[c], w(c))

    for c in range(8):
        orth(c)
    quad[blk] = gm_ref[...]
    pl.semaphore_wait(barrier, len(peers))

    quads = [push(quad.at[blk], quad.at[blk], peer) for peer in (zup, zdown, zfar)]
    u_up = push(pack_ref, block(1, blk, 0, 8), zup)
    u_down = push(pack_ref, block(1, blk, 0, 8), zdown)
    sides = [push(pack_ref, block(0, blk, 0, 8), right), push(pack_ref, block(2, blk, 0, 8), left)]
    for c in range(8, 16):
        orth(c)
    for c in range(16):
        newleaf_ref[c] = nt(nn(u(c), lt_ref[c]), w(16 + c // 2))

    for c in quads:
        c.wait_recv()
    root = None
    for n in range(2):
        g_ref[2 * n] = quad[2 * n, :, 0:N]
        g_ref[2 * n + 1] = quad[2 * n + 1, :, 0:N]
        g = quad[2 * n, :, N:2 * N] + quad[2 * n + 1, :, N:2 * N]
        g_ref[4 + n] = g
        m = sandwich(it_ref[1 + n], g)
        root = m if root is None else root + m
    g_ref[6] = root
    octet[low] = sandwich(it_ref[0], root)
    octets = [push(octet.at[low], octet.at[low], peer) for peer in mid]

    below, above, beyond = (blk + 3) % 4, (blk + 1) % 4, (blk + 2) % 4
    u_up.wait_recv()
    half_up = push(block(1, below, 0, 4), block(1, below, 0, 4), zup)
    u_down.wait_recv()
    half_down = push(block(1, above, 4, 4), block(1, above, 4, 4), zdown)
    for b in (below, above):
        sides += [push(block(1, b, 0, 8), block(0, b, 0, 8), right), push(block(1, b, 0, 8), block(2, b, 0, 8), left)]

    done, at = [], 16
    for count in (8, 4, 2):
        for n in range(count):
            e = it_ref[4 * count - 1 + count * blk + n]
            done.append(nt(nn(u(at + n), e), w(at + count + n // 2)))
        at += count
    for c in range(7):
        all_t[blk, c] = jnp.concatenate([done[2 * c], done[2 * c + 1]], axis=1)
    t_up = push(all_t.at[blk], all_t.at[blk], zup)
    t_down = push(all_t.at[blk], all_t.at[blk], zdown)

    for c in octets:
        c.wait_recv()
    first = [octet[2 * n] + octet[2 * n + 1] for n in range(4)]
    g_ref[7] = octet[low // 2 * 2] + octet[low // 2 * 2 + 1]
    images = [sandwich(up_ref[high * 8 + 2 * n], first[n]) for n in range(4)]
    second = [images[2 * n] + images[2 * n + 1] for n in range(2)]
    g_ref[8] = jnp.where(low < 4, second[0], second[1])
    images = [sandwich(up_ref[high * 8 + 4 * n + 1], second[n]) for n in range(2)]
    third = images[0] + images[1]
    g_ref[9] = third
    four[high] = sandwich(up_ref[high * 8 + 3], third)
    fours = [push(four.at[high], four.at[high], peer) for peer in far]

    half_up.wait_recv()
    half_down.wait_recv()
    sides += [push(block(1, beyond, 0, 8), block(0, beyond, 0, 8), right),
              push(block(1, beyond, 0, 8), block(2, beyond, 0, 8), left)]

    lane = lax.broadcasted_iota(jnp.int32, (N, 2 * N), 1)
    lower = lane < N
    fetch.wait()

    def turn(a, _):
        x = jnp.concatenate([buf[a, :, 0:128], buf[a, :, 128:256]], axis=0)
        s[pl.ds(a, 128, stride=N), :] = x.T
        return 0
    lax.fori_loop(0, N, turn, 0, unroll=8)

    for c in fours:
        c.wait_recv()
    fourth = [four[2 * n] + four[2 * n + 1] for n in range(2)]
    g_ref[10] = jnp.where(high < 2, fourth[0], fourth[1])
    images = [sandwich(up_ref[16 * n + 7], fourth[n]) for n in range(2)]
    for n in range(11, 16):
        g_ref[n] = images[0] + images[1]

    t_up.wait_recv()
    t_half_up = push(all_t.at[below, pl.ds(0, 4)], all_t.at[below, pl.ds(0, 4)], zup)
    t_down.wait_recv()
    t_half_down = push(all_t.at[above, pl.ds(4, 3)], all_t.at[above, pl.ds(4, 3)], zdown)

    def prepare(p, _):
        h, l, hr, lr = cut(all_u[p])
        cols[2 * p] = jnp.concatenate([jnp.where(lower, h, hr), jnp.where(lower, l, lr)], axis=1).astype(BF)
        cols[2 * p + 1] = jnp.concatenate([jnp.where(lower, hr, h), jnp.where(lower, lr, l)], axis=1).astype(BF)
        return 0

    def prepare_rows(p, _):
        h, l, hr, lr = cut(all_u[32 + p])
        rows[2 * p] = jnp.where(lower, h, lr).astype(BF)
        rows[2 * p + 1] = jnp.where(lower, hr, l).astype(BF)
        return 0
    own_u.wait()
    lax.fori_loop(0, 32, prepare_rows, 0, unroll=8)
    lax.fori_loop(32, 64, prepare, 0, unroll=8)
    for c in sides:
        c.wait_recv()
    lax.fori_loop(0, 32, prepare, 0, unroll=8)
    lax.fori_loop(64, 96, prepare, 0, unroll=8)

    base = leaf * 64

    def slot(k, d):
        i = jnp.clip(table_ref[0, k] - base, 0, 63)
        j = jnp.clip(table_ref[1, k] - base + 64, 0, 191)
        d = d.astype(BF)
        y = lax.dot_general(jnp.concatenate([d, d], axis=1), cols[j], (((1,), (1,)), ((), ())), preferred_element_type=F32)
        h = y.astype(BF)
        l = (y - h.astype(F32)).astype(BF)
        x = rows[i]
        return lax.dot_general(jnp.concatenate([x, x], axis=1), jnp.concatenate([h, h, l, l], axis=0),
                               (((1,), (0,)), ((), ())), preferred_element_type=F32)

    def both(k, _):
        at = pl.ds(pl.multiple_of(k * N, N), N)
        h, l, hr, lr = cut(s[at, :])
        r[at, :] = jnp.concatenate([slot(k, jnp.where(lower, h, lr)), slot(k + 128, jnp.where(lower, hr, l))], axis=1)
        return 0
    lax.fori_loop(0, 128, both, 0, unroll=16)

    live = count_ref[0]

    def back(a, _):
        x = r[pl.ds(a, 128, stride=N), :].T
        buf[a, :, 0:128] = jnp.where(lane < live, x[:N], F32(0))
        buf[a, :, 128:256] = jnp.where(lane + 128 < live, x[N:], F32(0))
        return 0
    stores = []
    for q in range(4):
        lax.fori_loop(16 * q, 16 * q + 16, back, 0, unroll=8)
        part = pl.ds(16 * q, 16)
        c = pltpu.make_async_copy(buf.at[part], out_ref.at[part], local_sem.at[2 + q])
        c.start()
        stores.append(c)

    t_half_up.wait_recv()
    t_half_down.wait_recv()
    for b in range(4):
        at = 0
        for count in (8, 4, 2):
            for n in range(count):
                inner_ref[4 * count - 8 + count * b + n] = all_t[b, at // 2, :, at % 2 * N:at % 2 * N + N]
                at += 1
    for c in used:
        c.wait_send()
    for c in stores:
        c.wait()


def run_middle(pairs, counts, gm, pack, u, w, basis, lt, it, up, coupling):
    vm = pl.BlockSpec(memory_space=pltpu.VMEM)
    sm = pl.BlockSpec(memory_space=pltpu.SMEM)
    hbm = pl.BlockSpec(memory_space=pl.ANY)
    sd = jax.ShapeDtypeStruct
    return pl.pallas_call(
        middle,
        out_shape=(sd((16, N, N), F32), sd((16, N, N), F32), sd((16, N, N), F32), sd((56, N, N), F32), sd((N, N, 256), F32)),
        in_specs=[sm, sm] + [vm] * 8 + [hbm],
        out_specs=(vm, vm, vm, vm, hbm),
        scratch_shapes=[
            pltpu.VMEM((N, N, 256), F32), pltpu.VMEM((128 * N, 2 * N), F32), pltpu.VMEM((128 * N, 2 * N), F32),
            pltpu.VMEM((192, N, 4 * N), BF), pltpu.VMEM((64, N, 2 * N), BF),
            pltpu.VMEM((96, N, 2 * N), F32), pltpu.VMEM((4, 7, N, 2 * N), F32),
            pltpu.VMEM((4, N, 2 * N), F32), pltpu.VMEM((8, N, N), F32), pltpu.VMEM((4, N, N), F32),
            pltpu.SemaphoreType.DMA((COPIES,)), pltpu.SemaphoreType.DMA((COPIES,)), pltpu.SemaphoreType.DMA((6,)),
        ],
        compiler_params=pltpu.CompilerParams(collective_id=0, has_side_effects=True, vmem_limit_bytes=58 * 2**20),
    )(pairs.T, counts, gm, pack, u, w, basis, lt, it, up, jnp.transpose(coupling, (1, 2, 0)))


def upper_factors(g_ref, it_ref, up_ref, pos_ref, orth_ref, leaf_ref, inner_ref, proj_ref,
                  orth_out, leaf_out, inner_out, proj_out, upper_ref, a, w, u_all, w_all, head, sem):
    leaf = pos_ref[0]
    copies = [pltpu.make_async_copy(orth_ref, orth_out, sem.at[0]), pltpu.make_async_copy(leaf_ref, leaf_out, sem.at[1]),
              pltpu.make_async_copy(inner_ref, inner_out.at[pl.ds(7, 56)], sem.at[2])]
    for q in range(4):
        part = pl.ds(16 * q, 16)
        copies.append(pltpu.make_async_copy(proj_ref.at[part], proj_out.at[part], sem.at[3 + q]))
    for c in copies:
        c.start()
    factor_stack(g_ref, u_all, w_all, a, w, 16)

    def u(i):
        return u_all[pl.ds(i * N, N), :]

    def inverse(i):
        return w_all[pl.ds(i * N, N), :]

    head[0] = nt(nn(u(6), it_ref[0]), inverse(7))
    for n in range(2):
        head[1 + n] = nt(nn(u(4 + n), it_ref[1 + n]), inverse(6))
    for n in range(4):
        head[3 + n] = nt(nn(u(n), it_ref[3 + n]), inverse(4 + n // 2))
    last = pltpu.make_async_copy(head, inner_out.at[pl.ds(0, 7)], sem.at[7])
    last.start()
    level = jnp.where(leaf % 2 == 1, 1, jnp.where(leaf % 4 == 2, 2, jnp.where(leaf % 8 == 4, 3, jnp.where(leaf % 16 == 8, 4, 5))))
    carried = nn(u(6 + level), up_ref[jnp.maximum(leaf - 1, 0)])
    renewed = nt(carried, inverse(jnp.minimum(7 + level, 11)))
    upper_ref[0] = jnp.where(leaf == 0, u(11), jnp.where(leaf == 16, carried, renewed))
    for c in copies:
        c.wait()
    last.wait()


def run_upper_factors(g, it, up, pos, orth, new_leaf, inner, proj):
    vm = pl.BlockSpec(memory_space=pltpu.VMEM)
    hbm = pl.BlockSpec(memory_space=pl.ANY)
    sd = jax.ShapeDtypeStruct
    return pl.pallas_call(
        upper_factors,
        out_shape=(sd((16, N, N), F32), sd((16, N, N), F32), sd((63, N, N), F32), sd((N, N, 256), F32), sd((1, N, N), F32)),
        in_specs=[vm, vm, vm, pl.BlockSpec(memory_space=pltpu.SMEM)] + [hbm] * 4,
        out_specs=(hbm, hbm, hbm, hbm, vm),
        scratch_shapes=[pltpu.VMEM((N, N, LANES), F32)] * 2 + [pltpu.VMEM((16 * N, N), F32)] * 2 + [
            pltpu.VMEM((7, N, N), F32), pltpu.SemaphoreType.DMA((8,))],
        compiler_params=pltpu.CompilerParams(vmem_limit_bytes=40 * 2**20),
    )(g.reshape(16 * N, N), it, up, pos, orth, new_leaf, inner, proj)


def body(leaf_basis, leaf_transfer, inner_transfer, upper_transfer, coupling, pairs, counts):
    pos = jnp.stack([lax.axis_index("leaf"), lax.axis_index("blk")]).astype(jnp.int32)
    g1, gm = run_local_tree(pos, leaf_basis, leaf_transfer, inner_transfer)
    u, w, pack = run_lower_factors(g1)
    orth, new_leaf, g2, inner, proj = run_middle(
        pairs, counts, gm, pack, u, w, leaf_basis, leaf_transfer, inner_transfer, upper_transfer, coupling)
    orth, new_leaf, inner, proj, upper = run_upper_factors(
        g2, inner_transfer, upper_transfer, pos, orth, new_leaf, inner, proj)
    return orth, new_leaf, inner, upper, jnp.transpose(proj, (2, 0, 1))


def solution(mesh):
    in_specs = (
        P(("leaf", "blk"), None, None),
        P(("leaf", "blk"), None, None),
        P("leaf", None, None),
        P(),
        P(("leaf", "blk"), None, None),
        P(("leaf", "blk"), None),
        P(("leaf", "blk")),
    )
    out_specs = (
        P(("leaf", "blk"), None, None),
        P(("leaf", "blk"), None, None),
        P("leaf", None, None),
        P("leaf", None, None),
        P(("leaf", "blk"), None, None),
    )
    return jax.shard_map(body, mesh=mesh, in_specs=in_specs, out_specs=out_specs, check_vma=False)
```

```python
import jax
import jax.numpy as jnp
from jax import lax
from jax.experimental import pallas as pl
from jax.experimental.pallas import tpu as pltpu
from jax.sharding import PartitionSpec as P

HIGH = lax.Precision.HIGHEST
F32 = jnp.float32
N = 64


def nn(a, b):
    return lax.dot_general(a, b, (((1,), (0,)), ((), ())), precision=HIGH, preferred_element_type=F32)


def tn(a, b):
    return lax.dot_general(a, b, (((0,), (0,)), ((), ())), precision=HIGH, preferred_element_type=F32)


def nt(a, b):
    return lax.dot_general(a, b, (((1,), (1,)), ((), ())), precision=HIGH, preferred_element_type=F32)


def sandwich(e, g):
    return tn(e, nn(g, e))


LANES = 128
COPIES = 29
VMEM = 60 * 2**20


def eliminate(a_ref, w_ref):
    sub = lax.broadcasted_iota(jnp.int32, (8, LANES), 0)

    def bc(x, i):
        return jnp.broadcast_to(x[i:i + 1, :], (8, LANES))

    def panel(p):
        k0 = 8 * p
        d = [a_ref[k0 + i, k0:k0 + 8, :] for i in range(8)]
        r, coef = [], {}
        for k in range(8):
            piv = bc(d[k], k)
            y = lax.rsqrt(piv)
            y = y * (1.5 - 0.5 * piv * y * y)
            r.append(y)
            d[k] = d[k] * y
            for i in range(k + 1, 8):
                coef[k, i] = bc(d[k], i)
                d[i] = d[i] - coef[k, i] * d[k]
        for i in range(8):
            a_ref[k0 + i, k0:k0 + 8, :] = d[i]

        def solve(x):
            for k in range(8):
                x[k] = x[k] * r[k]
                for i in range(k + 1, 8):
                    x[i] = x[i] - coef[k, i] * x[k]
            return x

        for jb in range(p + 1, 8):
            x = solve([a_ref[k0 + i, 8 * jb:8 * jb + 8, :] for i in range(8)])
            for i in range(8):
                a_ref[k0 + i, 8 * jb:8 * jb + 8, :] = x[i]
        for jb in range(p + 1):
            if jb < p:
                x = [w_ref[k0 + i, 8 * jb:8 * jb + 8, :] for i in range(8)]
            else:
                x = [jnp.where(sub == i, F32(1), F32(0)) for i in range(8)]
            x = solve(x)
            for i in range(8):
                w_ref[k0 + i, 8 * jb:8 * jb + 8, :] = x[i]

    def trail(p, row, targets):
        k0 = 8 * p
        for g in range(0, len(targets), 2):
            group = targets[g:g + 2]
            acc = {}
            for t, (ref, jb, fresh) in enumerate(group):
                for i in range(8):
                    acc[t, i] = jnp.zeros((8, LANES), F32) if fresh else ref[row + i, 8 * jb:8 * jb + 8, :]
            for k in range(8):
                pivots = [ref[k0 + k, 8 * jb:8 * jb + 8, :] for ref, jb, _ in group]
                for i in range(8):
                    c = jnp.broadcast_to(a_ref[k0 + k, pl.ds(row + i, 1), :], (8, LANES))
                    for t in range(len(group)):
                        acc[t, i] = acc[t, i] - c * pivots[t]
            for t, (ref, jb, _) in enumerate(group):
                for i in range(8):
                    ref[row + i, 8 * jb:8 * jb + 8, :] = acc[t, i]

    for p in range(8):
        panel(p)
        middle_block = (p + 9) // 2
        for start, stop in ((p + 1, middle_block), (middle_block, 8)):
            targets = [(a_ref, jb, False) for jb in range(start, 8)] + [(w_ref, jb, jb == p) for jb in range(p + 1)]

            def step(ib, _):
                trail(p, 8 * ib, targets)
                return 0
            lax.fori_loop(start, stop, step, 0)


def factor_stack(g_ref, u_ref, w_ref, a, w, n):
    def load(k, _):
        a[k, :, 0:n] = g_ref[pl.ds(k, n, stride=N), :].T
        return 0
    lax.fori_loop(0, N, load, 0, unroll=8)
    eliminate(a, w)
    col = lax.broadcasted_iota(jnp.int32, (N, n), 0)

    def save(k, _):
        u_ref[pl.ds(k, n, stride=N), :] = jnp.where(col >= k, a[k, :, 0:n], F32(0)).T
        w_ref[pl.ds(k, n, stride=N), :] = jnp.where(col <= k, w[k, :, 0:n], F32(0)).T
        return 0
    lax.fori_loop(0, N, save, 0, unroll=8)


def lower(pos_ref, basis_ref, lt_ref, it_ref, gm_ref, u_ref, w_ref, pack_ref, gram, tmp, e, a, w, sem):
    blk = pos_ref[1]
    fetches = []
    for t, (count, at) in enumerate(((8, 0), (4, 8), (2, 12), (1, 14))):
        c = pltpu.make_async_copy(it_ref.at[pl.ds(4 * count - 1 + count * blk, count)], e.at[pl.ds(at, count)], sem.at[t])
        c.start()
        fetches.append(c)

    def keep(i, g):
        gram[i * N:i * N + N, :] = g

    for c in range(16):
        b = basis_ref[c]
        g = tn(b, b)
        keep(c, g)
        tmp[c] = sandwich(lt_ref[c], g)
    at, src = 16, 0
    for t, count in enumerate((8, 4, 2, 1)):
        fetches[t].wait()
        for n in range(count):
            g = tmp[src + 2 * n] + tmp[src + 2 * n + 1]
            keep(at + n, g)
            m = sandwich(e[at - 16 + n], g)
            if count == 1:
                gm_ref[...] = jnp.concatenate([g, m], axis=1)
                keep(31, g)
            else:
                tmp[src + 2 * count + n] = m
        src += 2 * count
        at += count
    factor_stack(gram, u_ref, w_ref, a, w, 32)
    for c in range(8):
        pack_ref[c] = jnp.concatenate([u_ref[2 * c * N:2 * c * N + N, :], u_ref[2 * c * N + N:2 * c * N + 2 * N, :]], axis=1)


def run_lower(pos, basis, lt, it):
    vm = pl.BlockSpec(memory_space=pltpu.VMEM)
    sd = jax.ShapeDtypeStruct
    return pl.pallas_call(
        lower,
        out_shape=(sd((N, 2 * N), F32), sd((32 * N, N), F32), sd((32 * N, N), F32), sd((8, N, 2 * N), F32)),
        in_specs=[pl.BlockSpec(memory_space=pltpu.SMEM), vm, vm, pl.BlockSpec(memory_space=pl.ANY)],
        out_specs=(vm, vm, vm, vm),
        scratch_shapes=[pltpu.VMEM((32 * N, N), F32), pltpu.VMEM((32, N, N), F32), pltpu.VMEM((15, N, N), F32)]
        + [pltpu.VMEM((N, N, LANES), F32)] * 2 + [pltpu.SemaphoreType.DMA((4,))],
        compiler_params=pltpu.CompilerParams(vmem_limit_bytes=VMEM),
    )(pos, basis, lt, it)


BF = jnp.bfloat16


def split(x):
    h = x.astype(BF).astype(F32)
    return h, (x - h).astype(BF).astype(F32)


def cut(x):
    h, l = split(x)
    return h, l, pltpu.roll(h, N, 1), pltpu.roll(l, N, 1)


def middle(table_ref, count_ref, gm_hbm, pack_hbm, u_hbm, w_hbm, basis_hbm, lt_hbm, it_hbm, up_hbm, c_ref,
           orth_out, newleaf_out, g_ref, inner_out, out_ref,
           pack_ref, u_ref, w_ref, basis_ref, lt_ref, it_ref, up_ref, orth_ref, newleaf_ref, inner_ref, fetch_sem,
           buf, s, r, cols, rows, all_u, all_t, quad, octet, four, send_sem, recv_sem, local_sem):
    leaf, blk = lax.axis_index("leaf"), lax.axis_index("blk")
    low, high = leaf % 8, leaf // 8
    zup, zdown, zfar = [{"leaf": leaf, "blk": (blk + i) % 4} for i in (1, 3, 2)]
    right = {"leaf": (leaf + 1) % 32, "blk": blk}
    left = {"leaf": (leaf + 31) % 32, "blk": blk}
    mid = [{"leaf": high * 8 + (low + i) % 8, "blk": blk} for i in range(1, 8)]
    far = [{"leaf": (high + i) % 4 * 8 + low, "blk": blk} for i in range(1, 4)]
    peers = [zup, zdown, zfar, right, left] + mid + far
    barrier = pltpu.get_barrier_semaphore()
    for peer in peers:
        pl.semaphore_signal(barrier, inc=1, device_id=peer, device_id_type=pl.DeviceIdType.MESH)
    fetches = {}
    for i, (name, a, b) in enumerate((
            ("gm", gm_hbm, quad.at[blk]), ("pack", pack_hbm, pack_ref), ("w", w_hbm, w_ref), ("basis", basis_hbm, basis_ref),
            ("u", u_hbm, u_ref), ("lt", lt_hbm, lt_ref), ("it", it_hbm, it_ref), ("up", up_hbm, up_ref))):
        fetches[name] = pltpu.make_async_copy(a, b, fetch_sem.at[i])
        fetches[name].start()
    own_u = pltpu.make_async_copy(pack_hbm, all_u.at[pl.ds((4 + blk) * 8, 8)], local_sem.at[1])
    own_u.start()
    fetch = pltpu.make_async_copy(c_ref, buf, local_sem.at[0])
    fetch.start()
    used = []

    def push(src, dst, peer):
        i = len(used)
        c = pltpu.make_async_remote_copy(
            src_ref=src, dst_ref=dst, send_sem=send_sem.at[i], recv_sem=recv_sem.at[i],
            device_id=peer, device_id_type=pl.DeviceIdType.MESH)
        c.start()
        used.append(c)
        return c

    def block(d, b, start, count):
        return all_u.at[pl.ds((d * 4 + b) * 8 + start, count)]

    def u(i):
        return u_ref[i * N:i * N + N, :]

    def w(i):
        return w_ref[i * N:i * N + N, :]

    def orth(c):
        orth_ref[c] = nt(basis_ref[c], w(c))

    fetches["gm"].wait()
    fetches["pack"].wait()
    pl.semaphore_wait(barrier, len(peers))

    quads = [push(quad.at[blk], quad.at[blk], peer) for peer in (zup, zdown, zfar)]
    u_up = push(pack_ref, block(1, blk, 0, 8), zup)
    u_down = push(pack_ref, block(1, blk, 0, 8), zdown)
    sides = [push(pack_ref, block(0, blk, 0, 8), right), push(pack_ref, block(2, blk, 0, 8), left)]
    fetches["w"].wait()
    fetches["basis"].wait()
    for c in range(16):
        orth(c)
    fetches["u"].wait()
    fetches["lt"].wait()
    orth_store = pltpu.make_async_copy(orth_ref, orth_out, local_sem.at[6])
    orth_store.start()
    for c in range(8):
        x = jnp.concatenate([nn(u(2 * c), lt_ref[2 * c]), nn(u(2 * c + 1), lt_ref[2 * c + 1])], axis=0)
        x = nt(x, w(16 + c))
        newleaf_ref[2 * c] = x[:N]
        newleaf_ref[2 * c + 1] = x[N:]
    leaf_store = pltpu.make_async_copy(newleaf_ref, newleaf_out, local_sem.at[7])
    leaf_store.start()
    fetches["it"].wait()
    fetches["up"].wait()

    for c in quads:
        c.wait_recv()
    root = None
    for n in range(2):
        g_ref[2 * n] = quad[2 * n, :, 0:N]
        g_ref[2 * n + 1] = quad[2 * n + 1, :, 0:N]
        g = quad[2 * n, :, N:2 * N] + quad[2 * n + 1, :, N:2 * N]
        g_ref[4 + n] = g
        m = sandwich(it_ref[1 + n], g)
        root = m if root is None else root + m
    g_ref[6] = root
    octet[low] = sandwich(it_ref[0], root)
    octets = [push(octet.at[low], octet.at[low], peer) for peer in mid]

    below, above, beyond = (blk + 3) % 4, (blk + 1) % 4, (blk + 2) % 4
    u_up.wait_recv()
    half_up = push(block(1, below, 0, 4), block(1, below, 0, 4), zup)
    u_down.wait_recv()
    half_down = push(block(1, above, 4, 4), block(1, above, 4, 4), zdown)
    for b in (below, above):
        sides += [push(block(1, b, 0, 8), block(0, b, 0, 8), right), push(block(1, b, 0, 8), block(2, b, 0, 8), left)]

    done, at = [], 16
    for count in (8, 4, 2):
        for n in range(0, count, 2):
            first = 4 * count - 1 + count * blk + n
            x = jnp.concatenate([nn(u(at + n), it_ref[first]), nn(u(at + n + 1), it_ref[first + 1])], axis=0)
            x = nt(x, w(at + count + n // 2))
            done += [x[:N], x[N:]]
        at += count
    for c in range(7):
        all_t[blk, c] = jnp.concatenate([done[2 * c], done[2 * c + 1]], axis=1)
    t_up = push(all_t.at[blk], all_t.at[blk], zup)
    t_down = push(all_t.at[blk], all_t.at[blk], zdown)

    for c in octets:
        c.wait_recv()
    first = [octet[2 * n] + octet[2 * n + 1] for n in range(4)]
    g_ref[7] = octet[low // 2 * 2] + octet[low // 2 * 2 + 1]
    images = [sandwich(up_ref[high * 8 + 2 * n], first[n]) for n in range(4)]
    second = [images[2 * n] + images[2 * n + 1] for n in range(2)]
    g_ref[8] = jnp.where(low < 4, second[0], second[1])
    images = [sandwich(up_ref[high * 8 + 4 * n + 1], second[n]) for n in range(2)]
    third = images[0] + images[1]
    g_ref[9] = third
    four[high] = sandwich(up_ref[high * 8 + 3], third)
    fours = [push(four.at[high], four.at[high], peer) for peer in far]

    half_up.wait_recv()
    half_down.wait_recv()
    sides += [push(block(1, beyond, 0, 8), block(0, beyond, 0, 8), right),
              push(block(1, beyond, 0, 8), block(2, beyond, 0, 8), left)]

    lane = lax.broadcasted_iota(jnp.int32, (N, 2 * N), 1)
    lower = lane < N
    fetch.wait()

    def turn(a, _):
        x = jnp.concatenate([buf[a, :, 0:128], buf[a, :, 128:256]], axis=0)
        s[pl.ds(a, 128, stride=N), :] = x.T
        return 0
    lax.fori_loop(0, N, turn, 0, unroll=8)

    for c in fours:
        c.wait_recv()
    fourth = [four[2 * n] + four[2 * n + 1] for n in range(2)]
    g_ref[10] = jnp.where(high < 2, fourth[0], fourth[1])
    images = [sandwich(up_ref[16 * n + 7], fourth[n]) for n in range(2)]
    for n in range(11, 16):
        g_ref[n] = images[0] + images[1]

    t_up.wait_recv()
    t_half_up = push(all_t.at[below, pl.ds(0, 4)], all_t.at[below, pl.ds(0, 4)], zup)
    t_down.wait_recv()
    t_half_down = push(all_t.at[above, pl.ds(4, 3)], all_t.at[above, pl.ds(4, 3)], zdown)

    def prepare(p, _):
        h, l, hr, lr = cut(all_u[p])
        cols[2 * p] = jnp.concatenate([jnp.where(lower, h, hr), jnp.where(lower, l, lr)], axis=1).astype(BF)
        cols[2 * p + 1] = jnp.concatenate([jnp.where(lower, hr, h), jnp.where(lower, lr, l)], axis=1).astype(BF)
        return 0

    def prepare_rows(p, _):
        h, l, hr, lr = cut(all_u[32 + p])
        rows[2 * p] = jnp.where(lower, h, lr).astype(BF)
        rows[2 * p + 1] = jnp.where(lower, hr, l).astype(BF)
        return 0
    own_u.wait()
    lax.fori_loop(0, 32, prepare_rows, 0, unroll=8)
    lax.fori_loop(32, 64, prepare, 0, unroll=8)
    for c in sides:
        c.wait_recv()
    lax.fori_loop(0, 32, prepare, 0, unroll=8)
    lax.fori_loop(64, 96, prepare, 0, unroll=8)

    base = leaf * 64

    def slot(k, d):
        i = jnp.clip(table_ref[0, k] - base, 0, 63)
        j = jnp.clip(table_ref[1, k] - base + 64, 0, 191)
        d = d.astype(BF)
        y = lax.dot_general(jnp.concatenate([d, d], axis=1), cols[j], (((1,), (1,)), ((), ())), preferred_element_type=F32)
        h = y.astype(BF)
        l = (y - h.astype(F32)).astype(BF)
        x = rows[i]
        return lax.dot_general(jnp.concatenate([x, x], axis=1), jnp.concatenate([h, h, l, l], axis=0),
                               (((1,), (0,)), ((), ())), preferred_element_type=F32)

    def both(k, _):
        at = pl.ds(pl.multiple_of(k * N, N), N)
        h, l, hr, lr = cut(s[at, :])
        r[at, :] = jnp.concatenate([slot(k, jnp.where(lower, h, lr)), slot(k + 128, jnp.where(lower, hr, l))], axis=1)
        return 0
    lax.fori_loop(0, 128, both, 0, unroll=16)

    live = count_ref[0]

    def back(a, _):
        x = r[pl.ds(a, 128, stride=N), :].T
        buf[a, :, 0:128] = jnp.where(lane < live, x[:N], F32(0))
        buf[a, :, 128:256] = jnp.where(lane + 128 < live, x[N:], F32(0))
        return 0
    stores = []
    for q in range(4):
        lax.fori_loop(16 * q, 16 * q + 16, back, 0, unroll=8)
        part = pl.ds(16 * q, 16)
        c = pltpu.make_async_copy(buf.at[part], out_ref.at[part], local_sem.at[2 + q])
        c.start()
        stores.append(c)

    t_half_up.wait_recv()
    t_half_down.wait_recv()
    for b in range(4):
        at = 0
        for count in (8, 4, 2):
            for n in range(count):
                inner_ref[4 * count - 8 + count * b + n] = all_t[b, at // 2, :, at % 2 * N:at % 2 * N + N]
                at += 1
    inner_store = pltpu.make_async_copy(inner_ref, inner_out, local_sem.at[8])
    inner_store.start()
    for c in used:
        c.wait_send()
    for c in stores + [orth_store, leaf_store, inner_store]:
        c.wait()


def run_middle(pairs, counts, gm, pack, u, w, basis, lt, it, up, coupling):
    vm = pl.BlockSpec(memory_space=pltpu.VMEM)
    sm = pl.BlockSpec(memory_space=pltpu.SMEM)
    hbm = pl.BlockSpec(memory_space=pl.ANY)
    sd = jax.ShapeDtypeStruct
    return pl.pallas_call(
        middle,
        out_shape=(sd((16, N, N), F32), sd((16, N, N), F32), sd((16, N, N), F32), sd((56, N, N), F32), sd((N, N, 256), F32)),
        in_specs=[sm, sm] + [hbm] * 9,
        out_specs=(hbm, hbm, vm, hbm, hbm),
        scratch_shapes=[
            pltpu.VMEM((8, N, 2 * N), F32), pltpu.VMEM((32 * N, N), F32), pltpu.VMEM((32 * N, N), F32),
            pltpu.VMEM((16, N, N), F32), pltpu.VMEM((16, N, N), F32), pltpu.VMEM((63, N, N), F32), pltpu.VMEM((31, N, N), F32),
            pltpu.VMEM((16, N, N), F32), pltpu.VMEM((16, N, N), F32), pltpu.VMEM((56, N, N), F32), pltpu.SemaphoreType.DMA((8,)),
            pltpu.VMEM((N, N, 256), F32), pltpu.VMEM((128 * N, 2 * N), F32), pltpu.VMEM((128 * N, 2 * N), F32),
            pltpu.VMEM((192, N, 4 * N), BF), pltpu.VMEM((64, N, 2 * N), BF),
            pltpu.VMEM((96, N, 2 * N), F32), pltpu.VMEM((4, 7, N, 2 * N), F32),
            pltpu.VMEM((4, N, 2 * N), F32), pltpu.VMEM((8, N, N), F32), pltpu.VMEM((4, N, N), F32),
            pltpu.SemaphoreType.DMA((COPIES,)), pltpu.SemaphoreType.DMA((COPIES,)), pltpu.SemaphoreType.DMA((9,)),
        ],
        compiler_params=pltpu.CompilerParams(collective_id=0, has_side_effects=True, vmem_limit_bytes=VMEM),
    )(pairs.T, counts, gm, pack, u, w, basis, lt, it, up, jnp.transpose(coupling, (1, 2, 0)))


def upper_factors(g_ref, it_hbm, up_hbm, pos_ref, orth_ref, leaf_ref, inner_ref, proj_ref,
                  orth_out, leaf_out, inner_out, proj_out, upper_ref, a, w, u_all, w_all, head, it_ref, up_ref, sem):
    leaf = pos_ref[0]
    fetches = [pltpu.make_async_copy(it_hbm.at[pl.ds(0, 7)], it_ref, sem.at[8]),
               pltpu.make_async_copy(up_hbm.at[pl.ds(jnp.maximum(leaf - 1, 0), 1)], up_ref, sem.at[9])]
    for c in fetches:
        c.start()
    copies = [pltpu.make_async_copy(orth_ref, orth_out, sem.at[0]), pltpu.make_async_copy(leaf_ref, leaf_out, sem.at[1]),
              pltpu.make_async_copy(inner_ref, inner_out.at[pl.ds(7, 56)], sem.at[2])]
    for q in range(4):
        part = pl.ds(16 * q, 16)
        copies.append(pltpu.make_async_copy(proj_ref.at[part], proj_out.at[part], sem.at[3 + q]))
    for c in copies:
        c.start()
    factor_stack(g_ref, u_all, w_all, a, w, 16)
    for c in fetches:
        c.wait()

    def u(i):
        return u_all[pl.ds(i * N, N), :]

    def inverse(i):
        return w_all[pl.ds(i * N, N), :]

    head[0] = nt(nn(u(6), it_ref[0]), inverse(7))
    for n in range(2):
        head[1 + n] = nt(nn(u(4 + n), it_ref[1 + n]), inverse(6))
    for n in range(4):
        head[3 + n] = nt(nn(u(n), it_ref[3 + n]), inverse(4 + n // 2))
    last = pltpu.make_async_copy(head, inner_out.at[pl.ds(0, 7)], sem.at[7])
    last.start()
    level = jnp.where(leaf % 2 == 1, 1, jnp.where(leaf % 4 == 2, 2, jnp.where(leaf % 8 == 4, 3, jnp.where(leaf % 16 == 8, 4, 5))))
    carried = nn(u(6 + level), up_ref[0])
    renewed = nt(carried, inverse(jnp.minimum(7 + level, 11)))
    upper_ref[0] = jnp.where(leaf == 0, u(11), jnp.where(leaf == 16, carried, renewed))
    for c in copies:
        c.wait()
    last.wait()


def run_upper_factors(g, it, up, pos, orth, new_leaf, inner, proj):
    vm = pl.BlockSpec(memory_space=pltpu.VMEM)
    hbm = pl.BlockSpec(memory_space=pl.ANY)
    sd = jax.ShapeDtypeStruct
    return pl.pallas_call(
        upper_factors,
        out_shape=(sd((16, N, N), F32), sd((16, N, N), F32), sd((63, N, N), F32), sd((N, N, 256), F32), sd((1, N, N), F32)),
        in_specs=[vm, hbm, hbm, pl.BlockSpec(memory_space=pltpu.SMEM)] + [hbm] * 4,
        out_specs=(hbm, hbm, hbm, hbm, vm),
        scratch_shapes=[pltpu.VMEM((N, N, LANES), F32)] * 2 + [pltpu.VMEM((16 * N, N), F32)] * 2 + [
            pltpu.VMEM((7, N, N), F32), pltpu.VMEM((7, N, N), F32), pltpu.VMEM((1, N, N), F32), pltpu.SemaphoreType.DMA((10,))],
        compiler_params=pltpu.CompilerParams(vmem_limit_bytes=VMEM),
    )(g.reshape(16 * N, N), it, up, pos, orth, new_leaf, inner, proj)


def body(leaf_basis, leaf_transfer, inner_transfer, upper_transfer, coupling, pairs, counts):
    pos = jnp.stack([lax.axis_index("leaf"), lax.axis_index("blk")]).astype(jnp.int32)
    gm, u, w, pack = run_lower(pos, leaf_basis, leaf_transfer, inner_transfer)
    orth, new_leaf, g2, inner, proj = run_middle(
        pairs, counts, gm, pack, u, w, leaf_basis, leaf_transfer, inner_transfer, upper_transfer, coupling)
    orth, new_leaf, inner, proj, upper = run_upper_factors(
        g2, inner_transfer, upper_transfer, pos, orth, new_leaf, inner, proj)
    return orth, new_leaf, inner, upper, jnp.transpose(proj, (2, 0, 1))


def solution(mesh):
    in_specs = (
        P(("leaf", "blk"), None, None),
        P(("leaf", "blk"), None, None),
        P("leaf", None, None),
        P(),
        P(("leaf", "blk"), None, None),
        P(("leaf", "blk"), None),
        P(("leaf", "blk")),
    )
    out_specs = (
        P(("leaf", "blk"), None, None),
        P(("leaf", "blk"), None, None),
        P("leaf", None, None),
        P("leaf", None, None),
        P(("leaf", "blk"), None, None),
    )
    return jax.shard_map(body, mesh=mesh, in_specs=in_specs, out_specs=out_specs, check_vma=False)
```

```python
import jax
import jax.numpy as jnp
from jax import lax
from jax.experimental import pallas as pl
from jax.experimental.pallas import tpu as pltpu
from jax.sharding import PartitionSpec as P

HIGH = lax.Precision.HIGHEST
F32 = jnp.float32
N = 64


def nn(a, b):
    return lax.dot_general(a, b, (((1,), (0,)), ((), ())), precision=HIGH, preferred_element_type=F32)


def tn(a, b):
    return lax.dot_general(a, b, (((0,), (0,)), ((), ())), precision=HIGH, preferred_element_type=F32)


def nt(a, b):
    return lax.dot_general(a, b, (((1,), (1,)), ((), ())), precision=HIGH, preferred_element_type=F32)


def sandwich(e, g):
    return tn(e, nn(g, e))


LANES = 128
COPIES = 29
VMEM = 60 * 2**20


def eliminate(a_ref, w_ref):
    sub = lax.broadcasted_iota(jnp.int32, (8, LANES), 0)

    def bc(x, i):
        return jnp.broadcast_to(x[i:i + 1, :], (8, LANES))

    def panel(p):
        k0 = 8 * p
        d = [a_ref[k0 + i, k0:k0 + 8, :] for i in range(8)]
        r, coef = [], {}
        for k in range(8):
            piv = bc(d[k], k)
            y = lax.rsqrt(piv)
            y = y * (1.5 - 0.5 * piv * y * y)
            r.append(y)
            d[k] = d[k] * y
            for i in range(k + 1, 8):
                coef[k, i] = bc(d[k], i)
                d[i] = d[i] - coef[k, i] * d[k]
        for i in range(8):
            a_ref[k0 + i, k0:k0 + 8, :] = d[i]

        def solve(x):
            for k in range(8):
                x[k] = x[k] * r[k]
                for i in range(k + 1, 8):
                    x[i] = x[i] - coef[k, i] * x[k]
            return x

        for jb in range(p + 1, 8):
            x = solve([a_ref[k0 + i, 8 * jb:8 * jb + 8, :] for i in range(8)])
            for i in range(8):
                a_ref[k0 + i, 8 * jb:8 * jb + 8, :] = x[i]
        for jb in range(p + 1):
            if jb < p:
                x = [w_ref[k0 + i, 8 * jb:8 * jb + 8, :] for i in range(8)]
            else:
                x = [jnp.where(sub == i, F32(1), F32(0)) for i in range(8)]
            x = solve(x)
            for i in range(8):
                w_ref[k0 + i, 8 * jb:8 * jb + 8, :] = x[i]

    def trail(p, row, targets):
        k0 = 8 * p
        for g in range(0, len(targets), 2):
            group = targets[g:g + 2]
            acc = {}
            for t, (ref, jb, fresh) in enumerate(group):
                for i in range(8):
                    acc[t, i] = jnp.zeros((8, LANES), F32) if fresh else ref[row + i, 8 * jb:8 * jb + 8, :]
            for k in range(8):
                pivots = [ref[k0 + k, 8 * jb:8 * jb + 8, :] for ref, jb, _ in group]
                for i in range(8):
                    c = jnp.broadcast_to(a_ref[k0 + k, pl.ds(row + i, 1), :], (8, LANES))
                    for t in range(len(group)):
                        acc[t, i] = acc[t, i] - c * pivots[t]
            for t, (ref, jb, _) in enumerate(group):
                for i in range(8):
                    ref[row + i, 8 * jb:8 * jb + 8, :] = acc[t, i]

    for p in range(8):
        panel(p)
        middle_block = (p + 9) // 2
        for start, stop in ((p + 1, middle_block), (middle_block, 8)):
            targets = [(a_ref, jb, False) for jb in range(start, 8)] + [(w_ref, jb, jb == p) for jb in range(p + 1)]

            def step(ib, _):
                trail(p, 8 * ib, targets)
                return 0
            lax.fori_loop(start, stop, step, 0)


def factor_stack(g_ref, uw_ref, a, w, n):
    def load(k, _):
        a[k] = jnp.concatenate([g_ref[pl.ds(k, n, stride=N), :]] * (LANES // n), axis=0).T
        return 0
    lax.fori_loop(0, N, load, 0, unroll=8)
    eliminate(a, w)
    col = lax.broadcasted_iota(jnp.int32, (N, LANES), 0)

    def save(k, _):
        x = jnp.concatenate([jnp.where(col >= k, a[k], F32(0)), jnp.where(col <= k, w[k], F32(0))], axis=0)
        uw_ref[pl.ds(k, n, stride=N), :] = x.T[:n]
        return 0
    lax.fori_loop(0, N, save, 0, unroll=8)


def lower(pos_ref, basis_ref, lt_ref, it_ref, gm_ref, pack_ref, tpack_ref, orth_ref, newleaf_ref, gram, tmp, e, a, winv, uw, sem):
    blk = pos_ref[1]
    fetches = []
    for t, (count, at) in enumerate(((8, 0), (4, 8), (2, 12), (1, 14))):
        c = pltpu.make_async_copy(it_ref.at[pl.ds(4 * count - 1 + count * blk, count)], e.at[pl.ds(at, count)], sem.at[t])
        c.start()
        fetches.append(c)

    def keep(i, g):
        gram[i * N:i * N + N, :] = g

    for c in range(16):
        b = basis_ref[c]
        g = tn(b, b)
        keep(c, g)
        tmp[c] = sandwich(lt_ref[c], g)
    at, src = 16, 0
    for t, count in enumerate((8, 4, 2, 1)):
        fetches[t].wait()
        for n in range(count):
            g = tmp[src + 2 * n] + tmp[src + 2 * n + 1]
            keep(at + n, g)
            m = sandwich(e[at - 16 + n], g)
            if count == 1:
                gm_ref[...] = jnp.concatenate([g, m], axis=1)
                keep(31, g)
            else:
                tmp[src + 2 * count + n] = m
        src += 2 * count
        at += count
    factor_stack(gram, uw, a, winv, 32)

    def u(i):
        return uw[i * N:i * N + N, 0:N]

    def w(i):
        return uw[i * N:i * N + N, N:2 * N]

    for c in range(8):
        pack_ref[c] = jnp.concatenate([u(2 * c), u(2 * c + 1)], axis=1)
    for c in range(16):
        orth_ref[c] = nt(basis_ref[c], w(c))
    for c in range(8):
        x = jnp.concatenate([nn(u(2 * c), lt_ref[2 * c]), nn(u(2 * c + 1), lt_ref[2 * c + 1])], axis=0)
        x = nt(x, w(16 + c))
        newleaf_ref[2 * c] = x[:N]
        newleaf_ref[2 * c + 1] = x[N:]
    at, pair = 16, 0
    for count in (8, 4, 2):
        for n in range(0, count, 2):
            x = jnp.concatenate([nn(u(at + n), e[at + n - 16]), nn(u(at + n + 1), e[at + n - 15])], axis=0)
            x = nt(x, w(at + count + n // 2))
            tpack_ref[pair] = jnp.concatenate([x[:N], x[N:]], axis=1)
            pair += 1
        at += count


def run_lower(pos, basis, lt, it):
    vm = pl.BlockSpec(memory_space=pltpu.VMEM)
    sd = jax.ShapeDtypeStruct
    return pl.pallas_call(
        lower,
        out_shape=(sd((N, 2 * N), F32), sd((8, N, 2 * N), F32), sd((7, N, 2 * N), F32), sd((16, N, N), F32), sd((16, N, N), F32)),
        in_specs=[pl.BlockSpec(memory_space=pltpu.SMEM), vm, vm, pl.BlockSpec(memory_space=pl.ANY)],
        out_specs=(vm,) * 5,
        scratch_shapes=[pltpu.VMEM((32 * N, N), F32), pltpu.VMEM((32, N, N), F32), pltpu.VMEM((15, N, N), F32)]
        + [pltpu.VMEM((N, N, LANES), F32)] * 2 + [pltpu.VMEM((32 * N, 2 * N), F32), pltpu.SemaphoreType.DMA((4,))],
        compiler_params=pltpu.CompilerParams(vmem_limit_bytes=VMEM),
    )(pos, basis, lt, it)


BF = jnp.bfloat16


def split(x):
    h = x.astype(BF).astype(F32)
    return h, (x - h).astype(BF).astype(F32)


def cut(x):
    h, l = split(x)
    return h, l, pltpu.roll(h, N, 1), pltpu.roll(l, N, 1)


def middle(gm_hbm, pack_hbm, tpack_hbm, it_hbm, up_hbm, u_out, t_out, head_ref, upper_ref,
           pack_ref, tpack_ref, it_ref, near_up, far_up, own_up, all_u, all_t, quad, octet, four, gram, a, winv, uw,
           send_sem, recv_sem, fetch_sem, store_sem):
    leaf, blk = lax.axis_index("leaf"), lax.axis_index("blk")
    low, high = leaf % 8, leaf // 8
    zup, zdown, zfar = [{"leaf": leaf, "blk": (blk + i) % 4} for i in (1, 3, 2)]
    right = {"leaf": (leaf + 1) % 32, "blk": blk}
    left = {"leaf": (leaf + 31) % 32, "blk": blk}
    mid = [{"leaf": high * 8 + (low + i) % 8, "blk": blk} for i in range(1, 8)]
    far = [{"leaf": (high + i) % 4 * 8 + low, "blk": blk} for i in range(1, 4)]
    peers = [zup, zdown, zfar, right, left] + mid + far
    barrier = pltpu.get_barrier_semaphore()
    for peer in peers:
        pl.semaphore_signal(barrier, inc=1, device_id=peer, device_id_type=pl.DeviceIdType.MESH)
    fetches = {}
    for i, (name, x, y) in enumerate((
            ("gm", gm_hbm, quad.at[blk]), ("pack", pack_hbm, pack_ref), ("it", it_hbm.at[pl.ds(0, 7)], it_ref),
            ("own", up_hbm.at[pl.ds(jnp.maximum(leaf - 1, 0), 1)], own_up), ("near", up_hbm.at[pl.ds(high * 8, 7)], near_up),
            ("far0", up_hbm.at[pl.ds(7, 1)], far_up.at[pl.ds(0, 1)]), ("far1", up_hbm.at[pl.ds(23, 1)], far_up.at[pl.ds(1, 1)]),
            ("tpack", tpack_hbm, tpack_ref))):
        fetches[name] = pltpu.make_async_copy(x, y, fetch_sem.at[i])
        fetches[name].start()
    used, stores = [], []

    def push(src, dst, peer):
        i = len(used)
        c = pltpu.make_async_remote_copy(
            src_ref=src, dst_ref=dst, send_sem=send_sem.at[i], recv_sem=recv_sem.at[i],
            device_id=peer, device_id_type=pl.DeviceIdType.MESH)
        c.start()
        used.append(c)
        return c

    def store(src, dst):
        c = pltpu.make_async_copy(src, dst, store_sem.at[len(stores)])
        c.start()
        stores.append(c)

    def block(d, b, start=0, count=8):
        return all_u.at[pl.ds((d * 4 + b) * 8 + start, count)]

    def keep(i, g):
        gram[i * N:i * N + N, :] = g

    fetches["gm"].wait()
    fetches["pack"].wait()
    pl.semaphore_wait(barrier, len(peers))
    quads = [push(quad.at[blk], quad.at[blk], peer) for peer in (zup, zdown, zfar)]
    u_up = push(pack_ref, block(1, blk), zup)
    u_down = push(pack_ref, block(1, blk), zdown)
    sides = [(push(pack_ref, block(0, blk), right), 0, blk), (push(pack_ref, block(2, blk), left), 2, blk)]
    fetches["tpack"].wait()
    store(pack_ref, u_out.at[pl.ds((4 + blk) * 8, 8)])
    store(tpack_ref, t_out.at[blk])

    fetches["it"].wait()
    for c in quads:
        c.wait_recv()
    root = None
    for n in range(2):
        keep(2 * n, quad[2 * n, :, 0:N])
        keep(2 * n + 1, quad[2 * n + 1, :, 0:N])
        g = quad[2 * n, :, N:2 * N] + quad[2 * n + 1, :, N:2 * N]
        keep(4 + n, g)
        m = sandwich(it_ref[1 + n], g)
        root = m if root is None else root + m
    keep(6, root)
    octet[low] = sandwich(it_ref[0], root)
    octets = [push(octet.at[low], octet.at[low], peer) for peer in mid]

    below, above, beyond = (blk + 3) % 4, (blk + 1) % 4, (blk + 2) % 4
    u_up.wait_recv()
    half_up = push(block(1, below, 0, 4), block(1, below, 0, 4), zup)
    u_down.wait_recv()
    half_down = push(block(1, above, 4, 4), block(1, above, 4, 4), zdown)
    for b in (below, above):
        sides += [(push(block(1, b), block(0, b), right), 0, b), (push(block(1, b), block(2, b), left), 2, b)]
        store(block(1, b), u_out.at[pl.ds((4 + b) * 8, 8)])

    for name in ("near", "far0", "far1", "own"):
        fetches[name].wait()
    for c in octets:
        c.wait_recv()
    first = [octet[2 * n] + octet[2 * n + 1] for n in range(4)]
    keep(7, octet[low // 2 * 2] + octet[low // 2 * 2 + 1])
    images = [sandwich(near_up[2 * n], first[n]) for n in range(4)]
    second = [images[2 * n] + images[2 * n + 1] for n in range(2)]
    keep(8, jnp.where(low < 4, second[0], second[1]))
    images = [sandwich(near_up[4 * n + 1], second[n]) for n in range(2)]
    third = images[0] + images[1]
    keep(9, third)
    four[high] = sandwich(near_up[3], third)
    fours = [push(four.at[high], four.at[high], peer) for peer in far]

    half_up.wait_recv()
    half_down.wait_recv()
    sides += [(push(block(1, beyond), block(0, beyond), right), 0, beyond), (push(block(1, beyond), block(2, beyond), left), 2, beyond)]
    store(block(1, beyond), u_out.at[pl.ds((4 + beyond) * 8, 8)])
    t_up = push(tpack_ref, all_t.at[blk], zup)
    t_down = push(tpack_ref, all_t.at[blk], zdown)

    for c in fours:
        c.wait_recv()
    fourth = [four[2 * n] + four[2 * n + 1] for n in range(2)]
    keep(10, jnp.where(high < 2, fourth[0], fourth[1]))
    images = [sandwich(far_up[n], fourth[n]) for n in range(2)]
    for n in range(11, 16):
        keep(n, images[0] + images[1])
    factor_stack(gram, uw, a, winv, 16)

    t_up.wait_recv()
    t_half_up = push(all_t.at[below, pl.ds(0, 4)], all_t.at[below, pl.ds(0, 4)], zup)
    t_down.wait_recv()
    t_half_down = push(all_t.at[above, pl.ds(4, 3)], all_t.at[above, pl.ds(4, 3)], zdown)
    for b in (below, above):
        store(all_t.at[b], t_out.at[b])

    def u(i):
        return uw[pl.ds(i * N, N), 0:N]

    def w(i):
        return uw[pl.ds(i * N, N), N:2 * N]

    head_ref[0] = nt(nn(u(6), it_ref[0]), w(7))
    for n in range(2):
        head_ref[1 + n] = nt(nn(u(4 + n), it_ref[1 + n]), w(6))
    for n in range(4):
        head_ref[3 + n] = nt(nn(u(n), it_ref[3 + n]), w(4 + n // 2))
    level = jnp.where(leaf % 2 == 1, 1, jnp.where(leaf % 4 == 2, 2, jnp.where(leaf % 8 == 4, 3, jnp.where(leaf % 16 == 8, 4, 5))))
    carried = nn(u(6 + level), own_up[0])
    renewed = nt(carried, w(jnp.minimum(7 + level, 11)))
    upper_ref[0] = jnp.where(leaf == 0, u(11), jnp.where(leaf == 16, carried, renewed))

    for c, d, b in sides:
        c.wait_recv()
        store(block(d, b), u_out.at[pl.ds((d * 4 + b) * 8, 8)])
    t_half_up.wait_recv()
    t_half_down.wait_recv()
    store(all_t.at[beyond], t_out.at[beyond])
    for c in used:
        c.wait_send()
    for c in stores:
        c.wait()


def run_middle(gm, pack, tpack, it, up):
    vm = pl.BlockSpec(memory_space=pltpu.VMEM)
    hbm = pl.BlockSpec(memory_space=pl.ANY)
    sd = jax.ShapeDtypeStruct
    return pl.pallas_call(
        middle,
        out_shape=(sd((96, N, 2 * N), F32), sd((4, 7, N, 2 * N), F32), sd((7, N, N), F32), sd((1, N, N), F32)),
        in_specs=[hbm] * 5,
        out_specs=(hbm, hbm, vm, vm),
        scratch_shapes=[
            pltpu.VMEM((8, N, 2 * N), F32), pltpu.VMEM((7, N, 2 * N), F32), pltpu.VMEM((7, N, N), F32),
            pltpu.VMEM((7, N, N), F32), pltpu.VMEM((2, N, N), F32), pltpu.VMEM((1, N, N), F32),
            pltpu.VMEM((96, N, 2 * N), F32), pltpu.VMEM((4, 7, N, 2 * N), F32),
            pltpu.VMEM((4, N, 2 * N), F32), pltpu.VMEM((8, N, N), F32), pltpu.VMEM((4, N, N), F32),
            pltpu.VMEM((16 * N, N), F32), pltpu.VMEM((N, N, LANES), F32), pltpu.VMEM((N, N, LANES), F32),
            pltpu.VMEM((16 * N, 2 * N), F32),
            pltpu.SemaphoreType.DMA((COPIES,)), pltpu.SemaphoreType.DMA((COPIES,)), pltpu.SemaphoreType.DMA((8,)),
            pltpu.SemaphoreType.DMA((16,)),
        ],
        compiler_params=pltpu.CompilerParams(collective_id=0, has_side_effects=True, vmem_limit_bytes=VMEM),
    )(gm, pack, tpack, it, up)


def project(table_ref, count_ref, pos_ref, c_ref, u_hbm, t_hbm, head_hbm, inner_out, out_ref,
            buf, s, r, cols, rows, all_u, all_t, inner_ref, fetch_sem, store_sem):
    fetches = []
    for q in range(4):
        part = pl.ds(16 * q, 16)
        fetches.append(pltpu.make_async_copy(c_ref.at[part], buf.at[part], fetch_sem.at[q]))
    fetches.append(pltpu.make_async_copy(u_hbm, all_u, fetch_sem.at[4]))
    fetches.append(pltpu.make_async_copy(t_hbm, all_t, fetch_sem.at[5]))
    fetches.append(pltpu.make_async_copy(head_hbm, inner_ref.at[pl.ds(0, 7)], fetch_sem.at[6]))
    for c in fetches:
        c.start()
    lane = lax.broadcasted_iota(jnp.int32, (N, 2 * N), 1)
    lower_lanes = lane < N

    def turn(k, _):
        x = jnp.concatenate([buf[k, :, 0:128], buf[k, :, 128:256]], axis=0)
        s[pl.ds(k, 128, stride=N), :] = x.T
        return 0
    for q in range(4):
        fetches[q].wait()
        lax.fori_loop(16 * q, 16 * q + 16, turn, 0, unroll=8)

    def prepare(p, _):
        h, l, hr, lr = cut(all_u[p])
        cols[2 * p] = jnp.concatenate([jnp.where(lower_lanes, h, hr), jnp.where(lower_lanes, l, lr)], axis=1).astype(BF)
        cols[2 * p + 1] = jnp.concatenate([jnp.where(lower_lanes, hr, h), jnp.where(lower_lanes, lr, l)], axis=1).astype(BF)
        return 0

    def prepare_rows(p, _):
        h, l, hr, lr = cut(all_u[32 + p])
        rows[2 * p] = jnp.where(lower_lanes, h, lr).astype(BF)
        rows[2 * p + 1] = jnp.where(lower_lanes, hr, l).astype(BF)
        return 0
    fetches[4].wait()
    lax.fori_loop(0, 96, prepare, 0, unroll=8)
    lax.fori_loop(0, 32, prepare_rows, 0, unroll=8)

    fetches[5].wait()
    fetches[6].wait()
    for b in range(4):
        at = 0
        for count in (8, 4, 2):
            for n in range(count):
                inner_ref[4 * count - 1 + count * b + n] = all_t[b, at // 2, :, at % 2 * N:at % 2 * N + N]
                at += 1
    stores = [pltpu.make_async_copy(inner_ref, inner_out, store_sem.at[4])]
    stores[0].start()
    base = pos_ref[0] * 64

    def slot(k, d):
        i = jnp.clip(table_ref[0, k] - base, 0, 63)
        j = jnp.clip(table_ref[1, k] - base + 64, 0, 191)
        d = d.astype(BF)
        y = lax.dot_general(jnp.concatenate([d, d], axis=1), cols[j], (((1,), (1,)), ((), ())), preferred_element_type=F32)
        h = y.astype(BF)
        l = (y - h.astype(F32)).astype(BF)
        x = rows[i]
        return lax.dot_general(jnp.concatenate([x, x], axis=1), jnp.concatenate([h, h, l, l], axis=0),
                               (((1,), (0,)), ((), ())), preferred_element_type=F32)

    def both(k, _):
        at = pl.ds(pl.multiple_of(k * N, N), N)
        h, l, hr, lr = cut(s[at, :])
        r[at, :] = jnp.concatenate([slot(k, jnp.where(lower_lanes, h, lr)), slot(k + 128, jnp.where(lower_lanes, hr, l))], axis=1)
        return 0
    lax.fori_loop(0, 128, both, 0, unroll=32)

    live = count_ref[0]

    def back(k, _):
        x = r[pl.ds(k, 128, stride=N), :].T
        buf[k, :, 0:128] = jnp.where(lane < live, x[:N], F32(0))
        buf[k, :, 128:256] = jnp.where(lane + 128 < live, x[N:], F32(0))
        return 0
    for q in range(4):
        lax.fori_loop(16 * q, 16 * q + 16, back, 0, unroll=8)
        part = pl.ds(16 * q, 16)
        c = pltpu.make_async_copy(buf.at[part], out_ref.at[part], store_sem.at[q])
        c.start()
        stores.append(c)
    for c in stores:
        c.wait()


def run_project(pairs, counts, pos, coupling, u, t, head):
    sm = pl.BlockSpec(memory_space=pltpu.SMEM)
    hbm = pl.BlockSpec(memory_space=pl.ANY)
    sd = jax.ShapeDtypeStruct
    inner, out = pl.pallas_call(
        project,
        out_shape=(sd((63, N, N), F32), sd((N, N, 256), F32)),
        in_specs=[sm, sm, sm, hbm, hbm, hbm, hbm],
        out_specs=(hbm, hbm),
        scratch_shapes=[
            pltpu.VMEM((N, N, 256), F32), pltpu.VMEM((128 * N, 2 * N), F32), pltpu.VMEM((128 * N, 2 * N), F32),
            pltpu.VMEM((192, N, 4 * N), BF), pltpu.VMEM((64, N, 2 * N), BF),
            pltpu.VMEM((96, N, 2 * N), F32), pltpu.VMEM((4, 7, N, 2 * N), F32), pltpu.VMEM((63, N, N), F32),
            pltpu.SemaphoreType.DMA((7,)), pltpu.SemaphoreType.DMA((5,)),
        ],
        compiler_params=pltpu.CompilerParams(vmem_limit_bytes=VMEM),
    )(pairs.T, counts, pos, jnp.transpose(coupling, (1, 2, 0)), u, t, head)
    return inner, jnp.transpose(out, (2, 0, 1))


def body(leaf_basis, leaf_transfer, inner_transfer, upper_transfer, coupling, pairs, counts):
    pos = jnp.stack([lax.axis_index("leaf"), lax.axis_index("blk")]).astype(jnp.int32)
    gm, pack, tpack, orth, new_leaf = run_lower(pos, leaf_basis, leaf_transfer, inner_transfer)
    all_u, all_t, head, upper = run_middle(gm, pack, tpack, inner_transfer, upper_transfer)
    inner, out = run_project(pairs, counts, pos, coupling, all_u, all_t, head)
    return orth, new_leaf, inner, upper, out


def solution(mesh):
    in_specs = (
        P(("leaf", "blk"), None, None),
        P(("leaf", "blk"), None, None),
        P("leaf", None, None),
        P(),
        P(("leaf", "blk"), None, None),
        P(("leaf", "blk"), None),
        P(("leaf", "blk")),
    )
    out_specs = (
        P(("leaf", "blk"), None, None),
        P(("leaf", "blk"), None, None),
        P("leaf", None, None),
        P("leaf", None, None),
        P(("leaf", "blk"), None, None),
    )
    return jax.shard_map(body, mesh=mesh, in_specs=in_specs, out_specs=out_specs, check_vma=False)
```

```python
import jax
import jax.numpy as jnp
from jax import lax
from jax.experimental import pallas as pl
from jax.experimental.pallas import tpu as pltpu
from jax.sharding import PartitionSpec as P

HIGH = lax.Precision.HIGHEST
F32 = jnp.float32
N = 64


def nn(a, b):
    return lax.dot_general(a, b, (((1,), (0,)), ((), ())), precision=HIGH, preferred_element_type=F32)


def tn(a, b):
    return lax.dot_general(a, b, (((0,), (0,)), ((), ())), precision=HIGH, preferred_element_type=F32)


def nt(a, b):
    return lax.dot_general(a, b, (((1,), (1,)), ((), ())), precision=HIGH, preferred_element_type=F32)


def sandwich(e, g):
    return tn(e, nn(g, e))


LANES = 128
COPIES = 29
VMEM = 60 * 2**20


def eliminate(a_ref, w_ref):
    sub = lax.broadcasted_iota(jnp.int32, (8, LANES), 0)

    def bc(x, i):
        return jnp.broadcast_to(x[i:i + 1, :], (8, LANES))

    def panel(p):
        k0 = 8 * p
        d = [a_ref[k0 + i, k0:k0 + 8, :] for i in range(8)]
        r, coef = [], {}
        for k in range(8):
            piv = bc(d[k], k)
            y = lax.rsqrt(piv)
            y = y * (1.5 - 0.5 * piv * y * y)
            r.append(y)
            d[k] = d[k] * y
            for i in range(k + 1, 8):
                coef[k, i] = bc(d[k], i)
                d[i] = d[i] - coef[k, i] * d[k]
        for i in range(8):
            a_ref[k0 + i, k0:k0 + 8, :] = d[i]

        def solve(x):
            for k in range(8):
                x[k] = x[k] * r[k]
                for i in range(k + 1, 8):
                    x[i] = x[i] - coef[k, i] * x[k]
            return x

        for jb in range(p + 1, 8):
            x = solve([a_ref[k0 + i, 8 * jb:8 * jb + 8, :] for i in range(8)])
            for i in range(8):
                a_ref[k0 + i, 8 * jb:8 * jb + 8, :] = x[i]
        for jb in range(p + 1):
            if jb < p:
                x = [w_ref[k0 + i, 8 * jb:8 * jb + 8, :] for i in range(8)]
            else:
                x = [jnp.where(sub == i, F32(1), F32(0)) for i in range(8)]
            x = solve(x)
            for i in range(8):
                w_ref[k0 + i, 8 * jb:8 * jb + 8, :] = x[i]

    def trail(p, row, targets):
        k0 = 8 * p
        for g in range(0, len(targets), 2):
            group = targets[g:g + 2]
            acc = {}
            for t, (ref, jb, fresh) in enumerate(group):
                for i in range(8):
                    acc[t, i] = jnp.zeros((8, LANES), F32) if fresh else ref[row + i, 8 * jb:8 * jb + 8, :]
            for k in range(8):
                pivots = [ref[k0 + k, 8 * jb:8 * jb + 8, :] for ref, jb, _ in group]
                for i in range(8):
                    c = jnp.broadcast_to(a_ref[k0 + k, pl.ds(row + i, 1), :], (8, LANES))
                    for t in range(len(group)):
                        acc[t, i] = acc[t, i] - c * pivots[t]
            for t, (ref, jb, _) in enumerate(group):
                for i in range(8):
                    ref[row + i, 8 * jb:8 * jb + 8, :] = acc[t, i]

    for p in range(8):
        panel(p)
        middle_block = (p + 9) // 2
        for start, stop in ((p + 1, middle_block), (middle_block, 8)):
            targets = [(a_ref, jb, False) for jb in range(start, 8)] + [(w_ref, jb, jb == p) for jb in range(p + 1)]

            def step(ib, _):
                trail(p, 8 * ib, targets)
                return 0
            lax.fori_loop(start, stop, step, 0)


def factor_stack(g_ref, uw_ref, a, w, n, loaded=None, eliminated=None):
    def load(k, _):
        a[k] = jnp.concatenate([g_ref[pl.ds(k, n, stride=N), :]] * (LANES // n), axis=0).T
        return 0
    lax.fori_loop(0, N, load, 0, unroll=8)
    if loaded is not None:
        loaded()
    eliminate(a, w)
    if eliminated is not None:
        eliminated()
    col = lax.broadcasted_iota(jnp.int32, (N, LANES), 0)

    def save(k, _):
        x = jnp.concatenate([jnp.where(col >= k, a[k], F32(0)), jnp.where(col <= k, w[k], F32(0))], axis=0)
        uw_ref[pl.ds(k, n, stride=N), :] = x.T[:n]
        return 0
    lax.fori_loop(0, N, save, 0, unroll=8)


BF = jnp.bfloat16


def split(x):
    h = x.astype(BF).astype(F32)
    return h, (x - h).astype(BF).astype(F32)


def cut(x):
    h, l = split(x)
    return h, l, pltpu.roll(h, N, 1), pltpu.roll(l, N, 1)


def tree(basis_hbm, lt_hbm, it_hbm, up_hbm, orth_out, newleaf_out, u_out, t_out, head_ref, upper_ref,
         basis_ref, lt_ref, e, tmp, orth_ref, newleaf_ref, gram_low, uw_low, pack_ref, tpack_ref, it_ref, near_up, far_up, own_up, all_u, all_t, quad, octet, four, gram, a, winv, uw,
           send_sem, recv_sem, fetch_sem, store_sem):
    leaf, blk = lax.axis_index("leaf"), lax.axis_index("blk")
    low, high = leaf % 8, leaf // 8
    zup, zdown, zfar = [{"leaf": leaf, "blk": (blk + i) % 4} for i in (1, 3, 2)]
    right = {"leaf": (leaf + 1) % 32, "blk": blk}
    left = {"leaf": (leaf + 31) % 32, "blk": blk}
    mid = [{"leaf": high * 8 + (low + i) % 8, "blk": blk} for i in range(1, 8)]
    far = [{"leaf": (high + i) % 4 * 8 + low, "blk": blk} for i in range(1, 4)]
    peers = [zup, zdown, zfar, right, left] + mid + far
    barrier = pltpu.get_barrier_semaphore()
    for peer in peers:
        pl.semaphore_signal(barrier, inc=1, device_id=peer, device_id_type=pl.DeviceIdType.MESH)
    fetches = {}
    wanted = [("basis", basis_hbm, basis_ref), ("lt", lt_hbm, lt_ref)]
    for count, at in ((8, 0), (4, 8), (2, 12), (1, 14)):
        wanted.append(("e%d" % count, it_hbm.at[pl.ds(4 * count - 1 + count * blk, count)], e.at[pl.ds(at, count)]))
    wanted += [
        ("it", it_hbm.at[pl.ds(0, 7)], it_ref), ("own", up_hbm.at[pl.ds(jnp.maximum(leaf - 1, 0), 1)], own_up),
        ("near", up_hbm.at[pl.ds(high * 8, 7)], near_up), ("far0", up_hbm.at[pl.ds(7, 1)], far_up.at[pl.ds(0, 1)]),
        ("far1", up_hbm.at[pl.ds(23, 1)], far_up.at[pl.ds(1, 1)])]
    for i, (name, x, y) in enumerate(wanted):
        fetches[name] = pltpu.make_async_copy(x, y, fetch_sem.at[i])
        fetches[name].start()
    used, stores = [], []

    def push(src, dst, peer):
        i = len(used)
        c = pltpu.make_async_remote_copy(
            src_ref=src, dst_ref=dst, send_sem=send_sem.at[i], recv_sem=recv_sem.at[i],
            device_id=peer, device_id_type=pl.DeviceIdType.MESH)
        c.start()
        used.append(c)
        return c

    def store(src, dst):
        c = pltpu.make_async_copy(src, dst, store_sem.at[len(stores)])
        c.start()
        stores.append(c)

    def block(d, b, start=0, count=8):
        return all_u.at[pl.ds((d * 4 + b) * 8 + start, count)]

    def keep(i, g):
        gram[i * N:i * N + N, :] = g

    fetches["basis"].wait()
    fetches["lt"].wait()
    for c in range(16):
        b = basis_ref[c]
        g = tn(b, b)
        gram_low[c * N:c * N + N, :] = g
        tmp[c] = sandwich(lt_ref[c], g)
    at, done = 16, 0
    for count in (8, 4, 2, 1):
        fetches["e%d" % count].wait()
        for n in range(count):
            g = tmp[done + 2 * n] + tmp[done + 2 * n + 1]
            gram_low[(at + n) * N:(at + n) * N + N, :] = g
            m = sandwich(e[at - 16 + n], g)
            if count == 1:
                quad[blk] = jnp.concatenate([g, m], axis=1)
                gram_low[31 * N:32 * N, :] = g
            else:
                tmp[done + 2 * count + n] = m
        done += 2 * count
        at += count
    pl.semaphore_wait(barrier, len(peers))
    quads = [push(quad.at[blk], quad.at[blk], peer) for peer in (zup, zdown, zfar)]
    octets = []

    def subtree_top():
        fetches["it"].wait()
        for c in quads:
            c.wait_recv()
        root = None
        for n in range(2):
            keep(2 * n, quad[2 * n, :, 0:N])
            keep(2 * n + 1, quad[2 * n + 1, :, 0:N])
            g = quad[2 * n, :, N:2 * N] + quad[2 * n + 1, :, N:2 * N]
            keep(4 + n, g)
            m = sandwich(it_ref[1 + n], g)
            root = m if root is None else root + m
        keep(6, root)
        octet[low] = sandwich(it_ref[0], root)
        octets.extend([push(octet.at[low], octet.at[low], peer) for peer in mid])

    factor_stack(gram_low, uw_low, a, winv, 32, eliminated=subtree_top)

    def u_low(i):
        return uw_low[i * N:i * N + N, 0:N]

    def w_low(i):
        return uw_low[i * N:i * N + N, N:2 * N]

    for c in range(8):
        pack_ref[c] = jnp.concatenate([u_low(2 * c), u_low(2 * c + 1)], axis=1)
    u_up = push(pack_ref, block(1, blk), zup)
    u_down = push(pack_ref, block(1, blk), zdown)
    sides = [(push(pack_ref, block(0, blk), right), 0, blk), (push(pack_ref, block(2, blk), left), 2, blk)]
    store(pack_ref, u_out.at[pl.ds((4 + blk) * 8, 8)])

    for c in range(16):
        orth_ref[c] = nt(basis_ref[c], w_low(c))
    store(orth_ref, orth_out)
    for c in range(8):
        x = jnp.concatenate([nn(u_low(2 * c), lt_ref[2 * c]), nn(u_low(2 * c + 1), lt_ref[2 * c + 1])], axis=0)
        x = nt(x, w_low(16 + c))
        newleaf_ref[2 * c] = x[:N]
        newleaf_ref[2 * c + 1] = x[N:]
    store(newleaf_ref, newleaf_out)

    for name in ("near", "far0", "far1", "own"):
        fetches[name].wait()
    for c in octets:
        c.wait_recv()
    first = [octet[2 * n] + octet[2 * n + 1] for n in range(4)]
    keep(7, octet[low // 2 * 2] + octet[low // 2 * 2 + 1])
    images = [sandwich(near_up[2 * n], first[n]) for n in range(4)]
    second = [images[2 * n] + images[2 * n + 1] for n in range(2)]
    keep(8, jnp.where(low < 4, second[0], second[1]))
    images = [sandwich(near_up[4 * n + 1], second[n]) for n in range(2)]
    third = images[0] + images[1]
    keep(9, third)
    four[high] = sandwich(near_up[3], third)
    fours = [push(four.at[high], four.at[high], peer) for peer in far]

    below, above, beyond = (blk + 3) % 4, (blk + 1) % 4, (blk + 2) % 4
    u_up.wait_recv()
    half_up = push(block(1, below, 0, 4), block(1, below, 0, 4), zup)
    u_down.wait_recv()
    half_down = push(block(1, above, 4, 4), block(1, above, 4, 4), zdown)
    for b in (below, above):
        sides += [(push(block(1, b), block(0, b), right), 0, b), (push(block(1, b), block(2, b), left), 2, b)]
        store(block(1, b), u_out.at[pl.ds((4 + b) * 8, 8)])

    at, pair = 16, 0
    for count in (8, 4, 2):
        for n in range(0, count, 2):
            x = jnp.concatenate([nn(u_low(at + n), e[at + n - 16]), nn(u_low(at + n + 1), e[at + n - 15])], axis=0)
            x = nt(x, w_low(at + count + n // 2))
            tpack_ref[pair] = jnp.concatenate([x[:N], x[N:]], axis=1)
            pair += 1
        at += count
    store(tpack_ref, t_out.at[blk])
    t_up = push(tpack_ref, all_t.at[blk], zup)
    t_down = push(tpack_ref, all_t.at[blk], zdown)

    for c in fours:
        c.wait_recv()
    fourth = [four[2 * n] + four[2 * n + 1] for n in range(2)]
    keep(10, jnp.where(high < 2, fourth[0], fourth[1]))
    images = [sandwich(far_up[n], fourth[n]) for n in range(2)]
    for n in range(11, 16):
        keep(n, images[0] + images[1])

    def opposite():
        half_up.wait_recv()
        half_down.wait_recv()
        sides.extend([(push(block(1, beyond), block(0, beyond), right), 0, beyond), (push(block(1, beyond), block(2, beyond), left), 2, beyond)])
        store(block(1, beyond), u_out.at[pl.ds((4 + beyond) * 8, 8)])

    factor_stack(gram, uw, a, winv, 16, loaded=opposite)

    t_up.wait_recv()
    t_half_up = push(all_t.at[below, pl.ds(0, 4)], all_t.at[below, pl.ds(0, 4)], zup)
    t_down.wait_recv()
    t_half_down = push(all_t.at[above, pl.ds(4, 3)], all_t.at[above, pl.ds(4, 3)], zdown)
    for b in (below, above):
        store(all_t.at[b], t_out.at[b])

    def u(i):
        return uw[pl.ds(i * N, N), 0:N]

    def w(i):
        return uw[pl.ds(i * N, N), N:2 * N]

    head_ref[0] = nt(nn(u(6), it_ref[0]), w(7))
    for n in range(2):
        head_ref[1 + n] = nt(nn(u(4 + n), it_ref[1 + n]), w(6))
    for n in range(4):
        head_ref[3 + n] = nt(nn(u(n), it_ref[3 + n]), w(4 + n // 2))
    level = jnp.where(leaf % 2 == 1, 1, jnp.where(leaf % 4 == 2, 2, jnp.where(leaf % 8 == 4, 3, jnp.where(leaf % 16 == 8, 4, 5))))
    carried = nn(u(6 + level), own_up[0])
    renewed = nt(carried, w(jnp.minimum(7 + level, 11)))
    upper_ref[0] = jnp.where(leaf == 0, u(11), jnp.where(leaf == 16, carried, renewed))

    for c, d, b in sides:
        c.wait_recv()
        store(block(d, b), u_out.at[pl.ds((d * 4 + b) * 8, 8)])
    t_half_up.wait_recv()
    t_half_down.wait_recv()
    store(all_t.at[beyond], t_out.at[beyond])
    for c in used:
        c.wait_send()
    for c in stores:
        c.wait()


def run_tree(basis, lt, it, up):
    vm = pl.BlockSpec(memory_space=pltpu.VMEM)
    hbm = pl.BlockSpec(memory_space=pl.ANY)
    sd = jax.ShapeDtypeStruct
    leaves = pltpu.VMEM((16, N, N), F32)
    lanes = pltpu.VMEM((N, N, LANES), F32)
    return pl.pallas_call(
        tree,
        out_shape=(sd((16, N, N), F32), sd((16, N, N), F32), sd((96, N, 2 * N), F32), sd((4, 7, N, 2 * N), F32),
                   sd((7, N, N), F32), sd((1, N, N), F32)),
        in_specs=[hbm] * 4,
        out_specs=(hbm, hbm, hbm, hbm, vm, vm),
        scratch_shapes=[
            leaves, leaves, pltpu.VMEM((15, N, N), F32), pltpu.VMEM((32, N, N), F32), leaves, leaves,
            pltpu.VMEM((32 * N, N), F32), pltpu.VMEM((32 * N, 2 * N), F32),
            pltpu.VMEM((8, N, 2 * N), F32), pltpu.VMEM((7, N, 2 * N), F32), pltpu.VMEM((7, N, N), F32),
            pltpu.VMEM((7, N, N), F32), pltpu.VMEM((2, N, N), F32), pltpu.VMEM((1, N, N), F32),
            pltpu.VMEM((96, N, 2 * N), F32), pltpu.VMEM((4, 7, N, 2 * N), F32),
            pltpu.VMEM((4, N, 2 * N), F32), pltpu.VMEM((8, N, N), F32), pltpu.VMEM((4, N, N), F32),
            pltpu.VMEM((16 * N, N), F32), lanes, lanes, pltpu.VMEM((16 * N, 2 * N), F32),
            pltpu.SemaphoreType.DMA((COPIES,)), pltpu.SemaphoreType.DMA((COPIES,)), pltpu.SemaphoreType.DMA((11,)),
            pltpu.SemaphoreType.DMA((18,)),
        ],
        compiler_params=pltpu.CompilerParams(collective_id=0, has_side_effects=True, vmem_limit_bytes=VMEM),
    )(basis, lt, it, up)


def project(table_ref, count_ref, c_ref, u_hbm, t_hbm, head_hbm, orth_hbm, leaf_hbm, upper_hbm,
            inner_out, out_ref, orth_out, leaf_out, upper_out, orth_ref, leaf_ref, upper_ref,
            buf, s, r, cols, rows, all_u, all_t, inner_ref, fetch_sem, store_sem):
    fetches = []
    for q in range(4):
        part = pl.ds(16 * q, 16)
        fetches.append(pltpu.make_async_copy(c_ref.at[part], buf.at[part], fetch_sem.at[q]))
    fetches.append(pltpu.make_async_copy(u_hbm, all_u, fetch_sem.at[4]))
    fetches.append(pltpu.make_async_copy(t_hbm, all_t, fetch_sem.at[5]))
    fetches.append(pltpu.make_async_copy(head_hbm, inner_ref.at[pl.ds(0, 7)], fetch_sem.at[6]))
    through = ((orth_hbm, orth_ref, orth_out), (leaf_hbm, leaf_ref, leaf_out), (upper_hbm, upper_ref, upper_out))
    for i, (x, y, _) in enumerate(through):
        fetches.append(pltpu.make_async_copy(x, y, fetch_sem.at[7 + i]))
    for c in fetches:
        c.start()
    lane = lax.broadcasted_iota(jnp.int32, (N, 2 * N), 1)
    lower_lanes = lane < N

    def turn(k, _):
        x = jnp.concatenate([buf[k, :, 0:128], buf[k, :, 128:256]], axis=0)
        s[pl.ds(k, 128, stride=N), :] = x.T
        return 0
    for q in range(4):
        fetches[q].wait()
        lax.fori_loop(16 * q, 16 * q + 16, turn, 0, unroll=8)

    def prepare(p, _):
        h, l, hr, lr = cut(all_u[p])
        cols[2 * p] = jnp.concatenate([jnp.where(lower_lanes, h, hr), jnp.where(lower_lanes, l, lr)], axis=1).astype(BF)
        cols[2 * p + 1] = jnp.concatenate([jnp.where(lower_lanes, hr, h), jnp.where(lower_lanes, lr, l)], axis=1).astype(BF)
        return 0

    def prepare_rows(p, _):
        h, l, hr, lr = cut(all_u[32 + p])
        rows[2 * p] = jnp.where(lower_lanes, h, lr).astype(BF)
        rows[2 * p + 1] = jnp.where(lower_lanes, hr, l).astype(BF)
        return 0
    fetches[4].wait()
    lax.fori_loop(0, 96, prepare, 0, unroll=8)
    lax.fori_loop(0, 32, prepare_rows, 0, unroll=8)

    fetches[5].wait()
    fetches[6].wait()
    for b in range(4):
        at = 0
        for count in (8, 4, 2):
            for n in range(count):
                inner_ref[4 * count - 1 + count * b + n] = all_t[b, at // 2, :, at % 2 * N:at % 2 * N + N]
                at += 1
    stores = [pltpu.make_async_copy(inner_ref, inner_out, store_sem.at[4])]
    stores[0].start()
    for i, (_, y, z) in enumerate(through):
        fetches[7 + i].wait()
        stores.append(pltpu.make_async_copy(y, z, store_sem.at[5 + i]))
        stores[-1].start()
    base = lax.axis_index("leaf") * 64

    def slot(k, d):
        i = jnp.clip(table_ref[0, k] - base, 0, 63)
        j = jnp.clip(table_ref[1, k] - base + 64, 0, 191)
        d = d.astype(BF)
        y = lax.dot_general(jnp.concatenate([d, d], axis=1), cols[j], (((1,), (1,)), ((), ())), preferred_element_type=F32)
        h = y.astype(BF)
        l = (y - h.astype(F32)).astype(BF)
        x = rows[i]
        return lax.dot_general(jnp.concatenate([x, x], axis=1), jnp.concatenate([h, h, l, l], axis=0),
                               (((1,), (0,)), ((), ())), preferred_element_type=F32)

    def both(k, _):
        at = pl.ds(pl.multiple_of(k * N, N), N)
        h, l, hr, lr = cut(s[at, :])
        r[at, :] = jnp.concatenate([slot(k, jnp.where(lower_lanes, h, lr)), slot(k + 128, jnp.where(lower_lanes, hr, l))], axis=1)
        return 0
    lax.fori_loop(0, 128, both, 0, unroll=32)

    live = count_ref[0]

    def back(k, _):
        x = r[pl.ds(k, 128, stride=N), :].T
        buf[k, :, 0:128] = jnp.where(lane < live, x[:N], F32(0))
        buf[k, :, 128:256] = jnp.where(lane + 128 < live, x[N:], F32(0))
        return 0
    for q in range(4):
        lax.fori_loop(16 * q, 16 * q + 16, back, 0, unroll=8)
        part = pl.ds(16 * q, 16)
        c = pltpu.make_async_copy(buf.at[part], out_ref.at[part], store_sem.at[q])
        c.start()
        stores.append(c)
    for c in stores:
        c.wait()


def run_project(pairs, counts, coupling, u, t, head, orth, new_leaf, upper):
    sm = pl.BlockSpec(memory_space=pltpu.SMEM)
    hbm = pl.BlockSpec(memory_space=pl.ANY)
    sd = jax.ShapeDtypeStruct
    leaves = pltpu.VMEM((16, N, N), F32)
    inner, out, orth, new_leaf, upper = pl.pallas_call(
        project,
        out_shape=(sd((63, N, N), F32), sd((N, N, 256), F32), sd((16, N, N), F32), sd((16, N, N), F32), sd((1, N, N), F32)),
        in_specs=[sm, sm] + [hbm] * 7,
        out_specs=(hbm,) * 5,
        scratch_shapes=[
            leaves, leaves, pltpu.VMEM((1, N, N), F32),
            pltpu.VMEM((N, N, 256), F32), pltpu.VMEM((128 * N, 2 * N), F32), pltpu.VMEM((128 * N, 2 * N), F32),
            pltpu.VMEM((192, N, 4 * N), BF), pltpu.VMEM((64, N, 2 * N), BF),
            pltpu.VMEM((96, N, 2 * N), F32), pltpu.VMEM((4, 7, N, 2 * N), F32), pltpu.VMEM((63, N, N), F32),
            pltpu.SemaphoreType.DMA((10,)), pltpu.SemaphoreType.DMA((8,)),
        ],
        compiler_params=pltpu.CompilerParams(vmem_limit_bytes=VMEM),
    )(pairs.T, counts, jnp.transpose(coupling, (1, 2, 0)), u, t, head, orth, new_leaf, upper)
    return orth, new_leaf, inner, upper, jnp.transpose(out, (2, 0, 1))


def body(leaf_basis, leaf_transfer, inner_transfer, upper_transfer, coupling, pairs, counts):
    orth, new_leaf, all_u, all_t, head, upper = run_tree(leaf_basis, leaf_transfer, inner_transfer, upper_transfer)
    return run_project(pairs, counts, coupling, all_u, all_t, head, orth, new_leaf, upper)


def solution(mesh):
    in_specs = (
        P(("leaf", "blk"), None, None),
        P(("leaf", "blk"), None, None),
        P("leaf", None, None),
        P(),
        P(("leaf", "blk"), None, None),
        P(("leaf", "blk"), None),
        P(("leaf", "blk")),
    )
    out_specs = (
        P(("leaf", "blk"), None, None),
        P(("leaf", "blk"), None, None),
        P("leaf", None, None),
        P("leaf", None, None),
        P(("leaf", "blk"), None, None),
    )
    return jax.shard_map(body, mesh=mesh, in_specs=in_specs, out_specs=out_specs, check_vma=False)
```

```python
import jax
import jax.numpy as jnp
from jax import lax
from jax.experimental import pallas as pl
from jax.experimental.pallas import tpu as pltpu
from jax.sharding import PartitionSpec as P

HIGH = lax.Precision.HIGHEST
F32 = jnp.float32
N = 64


def nn(a, b):
    return lax.dot_general(a, b, (((1,), (0,)), ((), ())), precision=HIGH, preferred_element_type=F32)


def tn(a, b):
    return lax.dot_general(a, b, (((0,), (0,)), ((), ())), precision=HIGH, preferred_element_type=F32)


def nt(a, b):
    return lax.dot_general(a, b, (((1,), (1,)), ((), ())), precision=HIGH, preferred_element_type=F32)


def sandwich(e, g):
    return tn(e, nn(g, e))


LANES = 128
COPIES = 29
VMEM = 60 * 2**20


def eliminate(a_ref, w_ref):
    sub = lax.broadcasted_iota(jnp.int32, (8, LANES), 0)

    def bc(x, i):
        return jnp.broadcast_to(x[i:i + 1, :], (8, LANES))

    def panel(p):
        k0 = 8 * p
        d = [a_ref[k0 + i, k0:k0 + 8, :] for i in range(8)]
        r, coef = [], {}
        for k in range(8):
            piv = bc(d[k], k)
            y = lax.rsqrt(piv)
            y = y * (1.5 - 0.5 * piv * y * y)
            r.append(y)
            d[k] = d[k] * y
            for i in range(k + 1, 8):
                coef[k, i] = bc(d[k], i)
                d[i] = d[i] - coef[k, i] * d[k]
        for i in range(8):
            a_ref[k0 + i, k0:k0 + 8, :] = d[i]

        def solve(x):
            for k in range(8):
                x[k] = x[k] * r[k]
                for i in range(k + 1, 8):
                    x[i] = x[i] - coef[k, i] * x[k]
            return x

        for jb in range(p + 1, 8):
            x = solve([a_ref[k0 + i, 8 * jb:8 * jb + 8, :] for i in range(8)])
            for i in range(8):
                a_ref[k0 + i, 8 * jb:8 * jb + 8, :] = x[i]
        for jb in range(p + 1):
            if jb < p:
                x = [w_ref[k0 + i, 8 * jb:8 * jb + 8, :] for i in range(8)]
            else:
                x = [jnp.where(sub == i, F32(1), F32(0)) for i in range(8)]
            x = solve(x)
            for i in range(8):
                w_ref[k0 + i, 8 * jb:8 * jb + 8, :] = x[i]

    def trail(p, row, targets):
        k0 = 8 * p
        for g in range(0, len(targets), 2):
            group = targets[g:g + 2]
            acc = {}
            for t, (ref, jb, fresh) in enumerate(group):
                for i in range(8):
                    acc[t, i] = jnp.zeros((8, LANES), F32) if fresh else ref[row + i, 8 * jb:8 * jb + 8, :]
            for k in range(8):
                pivots = [ref[k0 + k, 8 * jb:8 * jb + 8, :] for ref, jb, _ in group]
                for i in range(8):
                    c = jnp.broadcast_to(a_ref[k0 + k, pl.ds(row + i, 1), :], (8, LANES))
                    for t in range(len(group)):
                        acc[t, i] = acc[t, i] - c * pivots[t]
            for t, (ref, jb, _) in enumerate(group):
                for i in range(8):
                    ref[row + i, 8 * jb:8 * jb + 8, :] = acc[t, i]

    for p in range(8):
        panel(p)
        middle_block = (p + 9) // 2
        for start, stop in ((p + 1, middle_block), (middle_block, 8)):
            targets = [(a_ref, jb, False) for jb in range(start, 8)] + [(w_ref, jb, jb == p) for jb in range(p + 1)]

            def step(ib, _):
                trail(p, 8 * ib, targets)
                return 0
            lax.fori_loop(start, stop, step, 0)


def factor_stack(g_ref, uw_ref, a, w, n, loaded=None, eliminated=None):
    def load(k, _):
        a[k] = jnp.concatenate([g_ref[pl.ds(k, n, stride=N), :]] * (LANES // n), axis=0).T
        return 0
    lax.fori_loop(0, N, load, 0, unroll=8)
    if loaded is not None:
        loaded()
    eliminate(a, w)
    if eliminated is not None:
        eliminated()
    col = lax.broadcasted_iota(jnp.int32, (N, LANES), 0)

    def save(k, _):
        x = jnp.concatenate([jnp.where(col >= k, a[k], F32(0)), jnp.where(col <= k, w[k], F32(0))], axis=0)
        uw_ref[pl.ds(k, n, stride=N), :] = x.T[:n]
        return 0
    lax.fori_loop(0, N, save, 0, unroll=8)


BF = jnp.bfloat16


def split(x):
    h = x.astype(BF).astype(F32)
    return h, (x - h).astype(BF).astype(F32)


def cut(x):
    h, l = split(x)
    return h, l, pltpu.roll(h, N, 1), pltpu.roll(l, N, 1)


def tree(table_ref, count_ref, basis_hbm, lt_hbm, it_hbm, up_hbm, c_hbm, orth_out, newleaf_out, t_out, gram, out_ref,
         buf, s, r, cols, rows, basis_ref, lt_ref, e, tmp, orth_ref, newleaf_ref, gram_low, uw_low, pack_ref, tpack_ref, it_ref, near_up, far_up, all_u, all_t, quad, octet, four, a, winv,
           send_sem, recv_sem, fetch_sem, store_sem, own_sem):
    leaf, blk = lax.axis_index("leaf"), lax.axis_index("blk")
    low, high = leaf % 8, leaf // 8
    zup, zdown, zfar = [{"leaf": leaf, "blk": (blk + i) % 4} for i in (1, 3, 2)]
    right = {"leaf": (leaf + 1) % 32, "blk": blk}
    left = {"leaf": (leaf + 31) % 32, "blk": blk}
    mid = [{"leaf": high * 8 + (low + i) % 8, "blk": blk} for i in range(1, 8)]
    far = [{"leaf": (high + i) % 4 * 8 + low, "blk": blk} for i in range(1, 4)]
    peers = [zup, zdown, zfar, right, left] + mid + far
    barrier = pltpu.get_barrier_semaphore()
    for peer in peers:
        pl.semaphore_signal(barrier, inc=1, device_id=peer, device_id_type=pl.DeviceIdType.MESH)
    fetches = {}
    wanted = [("basis", basis_hbm, basis_ref), ("lt", lt_hbm, lt_ref)]
    for count, at in ((8, 0), (4, 8), (2, 12), (1, 14)):
        wanted.append(("e%d" % count, it_hbm.at[pl.ds(4 * count - 1 + count * blk, count)], e.at[pl.ds(at, count)]))
    wanted += [
        ("it", it_hbm.at[pl.ds(0, 3)], it_ref),
        ("near", up_hbm.at[pl.ds(high * 8, 7)], near_up), ("far0", up_hbm.at[pl.ds(7, 1)], far_up.at[pl.ds(0, 1)]),
        ("far1", up_hbm.at[pl.ds(23, 1)], far_up.at[pl.ds(1, 1)]), ("c", c_hbm, buf)]
    for i, (name, x, y) in enumerate(wanted):
        fetches[name] = pltpu.make_async_copy(x, y, fetch_sem.at[i])
        fetches[name].start()
    used, stores = [], []

    def push(src, dst, peer):
        i = len(used)
        c = pltpu.make_async_remote_copy(
            src_ref=src, dst_ref=dst, send_sem=send_sem.at[i], recv_sem=recv_sem.at[i],
            device_id=peer, device_id_type=pl.DeviceIdType.MESH)
        c.start()
        used.append(c)
        return c

    def store(src, dst):
        c = pltpu.make_async_copy(src, dst, store_sem.at[len(stores)])
        c.start()
        stores.append(c)

    def block(d, b, start=0, count=8):
        return all_u.at[pl.ds((d * 4 + b) * 8 + start, count)]

    def keep(i, g):
        gram[i * N:i * N + N, :] = g

    fetches["basis"].wait()
    fetches["lt"].wait()
    for c in range(16):
        b = basis_ref[c]
        g = tn(b, b)
        gram_low[c * N:c * N + N, :] = g
        tmp[c] = sandwich(lt_ref[c], g)
    at, done = 16, 0
    for count in (8, 4, 2, 1):
        fetches["e%d" % count].wait()
        for n in range(count):
            g = tmp[done + 2 * n] + tmp[done + 2 * n + 1]
            gram_low[(at + n) * N:(at + n) * N + N, :] = g
            m = sandwich(e[at - 16 + n], g)
            if count == 1:
                quad[blk] = jnp.concatenate([g, m], axis=1)
                gram_low[31 * N:32 * N, :] = g
            else:
                tmp[done + 2 * count + n] = m
        done += 2 * count
        at += count
    pl.semaphore_wait(barrier, len(peers))
    quads = [push(quad.at[blk], quad.at[blk], peer) for peer in (zup, zdown, zfar)]
    octets = []

    def subtree_top():
        fetches["it"].wait()
        for c in quads:
            c.wait_recv()
        root = None
        for n in range(2):
            keep(2 * n, quad[2 * n, :, 0:N])
            keep(2 * n + 1, quad[2 * n + 1, :, 0:N])
            g = quad[2 * n, :, N:2 * N] + quad[2 * n + 1, :, N:2 * N]
            keep(4 + n, g)
            m = sandwich(it_ref[1 + n], g)
            root = m if root is None else root + m
        keep(6, root)
        octet[low] = sandwich(it_ref[0], root)
        octets.extend([push(octet.at[low], octet.at[low], peer) for peer in mid])

    factor_stack(gram_low, uw_low, a, winv, 32, eliminated=subtree_top)

    def u_low(i):
        return uw_low[i * N:i * N + N, 0:N]

    def w_low(i):
        return uw_low[i * N:i * N + N, N:2 * N]

    for c in range(8):
        pack_ref[c] = jnp.concatenate([u_low(2 * c), u_low(2 * c + 1)], axis=1)
    own_u = pltpu.make_async_copy(pack_ref, block(1, blk), own_sem.at[0])
    own_u.start()
    u_up = push(pack_ref, block(1, blk), zup)
    u_down = push(pack_ref, block(1, blk), zdown)
    sides = [(push(pack_ref, block(0, blk), right), 0, blk), (push(pack_ref, block(2, blk), left), 2, blk)]
    for c in range(16):
        orth_ref[c] = nt(basis_ref[c], w_low(c))
    store(orth_ref, orth_out)
    for c in range(8):
        x = jnp.concatenate([nn(u_low(2 * c), lt_ref[2 * c]), nn(u_low(2 * c + 1), lt_ref[2 * c + 1])], axis=0)
        x = nt(x, w_low(16 + c))
        newleaf_ref[2 * c] = x[:N]
        newleaf_ref[2 * c + 1] = x[N:]
    store(newleaf_ref, newleaf_out)

    lane = lax.broadcasted_iota(jnp.int32, (N, 2 * N), 1)
    lower_lanes = lane < N

    def turn(k, _):
        x = jnp.concatenate([buf[k, :, 0:128], buf[k, :, 128:256]], axis=0)
        s[pl.ds(k, 128, stride=N), :] = x.T
        return 0
    fetches["c"].wait()
    lax.fori_loop(0, N, turn, 0, unroll=8)

    at, pair = 16, 0
    for count in (8, 4, 2):
        for n in range(0, count, 2):
            x = jnp.concatenate([nn(u_low(at + n), e[at + n - 16]), nn(u_low(at + n + 1), e[at + n - 15])], axis=0)
            x = nt(x, w_low(at + count + n // 2))
            tpack_ref[pair] = jnp.concatenate([x[:N], x[N:]], axis=1)
            pair += 1
        at += count
    store(tpack_ref, t_out.at[blk])

    below, above, beyond = (blk + 3) % 4, (blk + 1) % 4, (blk + 2) % 4

    def forward(b):
        sides.extend([(push(block(1, b), block(0, b), right), 0, b), (push(block(1, b), block(2, b), left), 2, b)])

    def prepare(p, _):
        h, l, hr, lr = cut(all_u[p])
        cols[2 * p] = jnp.concatenate([jnp.where(lower_lanes, h, hr), jnp.where(lower_lanes, l, lr)], axis=1).astype(BF)
        cols[2 * p + 1] = jnp.concatenate([jnp.where(lower_lanes, hr, h), jnp.where(lower_lanes, lr, l)], axis=1).astype(BF)
        return 0

    def prepare_rows(p, _):
        h, l, hr, lr = cut(all_u[32 + p])
        rows[2 * p] = jnp.where(lower_lanes, h, lr).astype(BF)
        rows[2 * p + 1] = jnp.where(lower_lanes, hr, l).astype(BF)
        return 0
    def split_block(d, b):
        first = (d * 4 + b) * 8
        if d == 1:
            lax.fori_loop(0, 8, lambda p, _: prepare_rows(b * 8 + p, _), 0, unroll=8)
        lax.fori_loop(0, 8, lambda p, _: prepare(first + p, _), 0, unroll=8)

    u_up.wait_recv()
    half_up = push(block(1, below, 0, 4), block(1, below, 0, 4), zup)
    u_down.wait_recv()
    half_down = push(block(1, above, 4, 4), block(1, above, 4, 4), zdown)
    forward(below)
    forward(above)
    t_up = push(tpack_ref, all_t.at[blk], zup)
    t_down = push(tpack_ref, all_t.at[blk], zdown)
    own_u.wait()
    for b in (blk, below, above):
        split_block(1, b)

    for name in ("near", "far0", "far1"):
        fetches[name].wait()
    for c in octets:
        c.wait_recv()
    first = [octet[2 * n] + octet[2 * n + 1] for n in range(4)]
    keep(7, octet[low // 2 * 2] + octet[low // 2 * 2 + 1])
    images = [sandwich(near_up[2 * n], first[n]) for n in range(4)]
    second = [images[2 * n] + images[2 * n + 1] for n in range(2)]
    keep(8, jnp.where(low < 4, second[0], second[1]))
    images = [sandwich(near_up[4 * n + 1], second[n]) for n in range(2)]
    third = images[0] + images[1]
    keep(9, third)
    four[high] = sandwich(near_up[3], third)
    fours = [push(four.at[high], four.at[high], peer) for peer in far]

    half_up.wait_recv()
    half_down.wait_recv()
    forward(beyond)
    split_block(1, beyond)
    t_up.wait_recv()
    t_half_up = push(all_t.at[below, pl.ds(0, 4)], all_t.at[below, pl.ds(0, 4)], zup)
    t_down.wait_recv()
    t_half_down = push(all_t.at[above, pl.ds(4, 3)], all_t.at[above, pl.ds(4, 3)], zdown)
    for b in (below, above):
        store(all_t.at[b], t_out.at[b])
    for c, d, b in sides:
        c.wait_recv()
        split_block(d, b)

    base = leaf * 64

    def slot(k, d):
        i = jnp.clip(table_ref[0, k] - base, 0, 63)
        j = jnp.clip(table_ref[1, k] - base + 64, 0, 191)
        d = d.astype(BF)
        y = lax.dot_general(jnp.concatenate([d, d], axis=1), cols[j], (((1,), (1,)), ((), ())), preferred_element_type=F32)
        h = y.astype(BF)
        l = (y - h.astype(F32)).astype(BF)
        x = rows[i]
        return lax.dot_general(jnp.concatenate([x, x], axis=1), jnp.concatenate([h, h, l, l], axis=0),
                               (((1,), (0,)), ((), ())), preferred_element_type=F32)

    def both(k, _):
        at = pl.ds(pl.multiple_of(k * N, N), N)
        h, l, hr, lr = cut(s[at, :])
        r[at, :] = jnp.concatenate([slot(k, jnp.where(lower_lanes, h, lr)), slot(k + 128, jnp.where(lower_lanes, hr, l))], axis=1)
        return 0
    lax.fori_loop(0, 128, both, 0, unroll=32)

    for c in fours:
        c.wait_recv()
    fourth = [four[2 * n] + four[2 * n + 1] for n in range(2)]
    keep(10, jnp.where(high < 2, fourth[0], fourth[1]))
    images = [sandwich(far_up[n], fourth[n]) for n in range(2)]
    for n in range(11, 16):
        keep(n, images[0] + images[1])

    live = count_ref[0]

    def back(k, _):
        x = r[pl.ds(k, 128, stride=N), :].T
        buf[k, :, 0:128] = jnp.where(lane < live, x[:N], F32(0))
        buf[k, :, 128:256] = jnp.where(lane + 128 < live, x[N:], F32(0))
        return 0
    for q in range(4):
        lax.fori_loop(16 * q, 16 * q + 16, back, 0, unroll=8)
        part = pl.ds(16 * q, 16)
        store(buf.at[part], out_ref.at[part])

    t_half_up.wait_recv()
    t_half_down.wait_recv()
    store(all_t.at[beyond], t_out.at[beyond])
    for c in used:
        c.wait_send()
    for c in stores:
        c.wait()


def run_tree(pairs, counts, basis, lt, it, up, coupling):
    vm = pl.BlockSpec(memory_space=pltpu.VMEM)
    sm = pl.BlockSpec(memory_space=pltpu.SMEM)
    hbm = pl.BlockSpec(memory_space=pl.ANY)
    sd = jax.ShapeDtypeStruct
    leaves = pltpu.VMEM((16, N, N), F32)
    lanes = pltpu.VMEM((N, N, LANES), F32)
    return pl.pallas_call(
        tree,
        out_shape=(sd((16, N, N), F32), sd((16, N, N), F32), sd((4, 7, N, 2 * N), F32), sd((16 * N, N), F32), sd((N, N, 256), F32)),
        in_specs=[sm, sm] + [hbm] * 5,
        out_specs=(hbm, hbm, hbm, vm, hbm),
        scratch_shapes=[
            pltpu.VMEM((N, N, 256), F32), pltpu.VMEM((128 * N, 2 * N), F32), pltpu.VMEM((128 * N, 2 * N), F32),
            pltpu.VMEM((192, N, 4 * N), BF), pltpu.VMEM((64, N, 2 * N), BF),
            leaves, leaves, pltpu.VMEM((15, N, N), F32), pltpu.VMEM((32, N, N), F32), leaves, leaves,
            pltpu.VMEM((32 * N, N), F32), pltpu.VMEM((32 * N, 2 * N), F32),
            pltpu.VMEM((8, N, 2 * N), F32), pltpu.VMEM((7, N, 2 * N), F32), pltpu.VMEM((3, N, N), F32),
            pltpu.VMEM((7, N, N), F32), pltpu.VMEM((2, N, N), F32),
            pltpu.VMEM((96, N, 2 * N), F32), pltpu.VMEM((4, 7, N, 2 * N), F32),
            pltpu.VMEM((4, N, 2 * N), F32), pltpu.VMEM((8, N, N), F32), pltpu.VMEM((4, N, N), F32), lanes, lanes,
            pltpu.SemaphoreType.DMA((COPIES,)), pltpu.SemaphoreType.DMA((COPIES,)), pltpu.SemaphoreType.DMA((11,)),
            pltpu.SemaphoreType.DMA((10,)), pltpu.SemaphoreType.DMA((1,)),
        ],
        compiler_params=pltpu.CompilerParams(collective_id=0, has_side_effects=True, vmem_limit_bytes=VMEM),
    )(pairs.T, counts, basis, lt, it, up, jnp.transpose(coupling, (1, 2, 0)))


def top(gram_hbm, it_hbm, up_hbm, orth_hbm, leaf_hbm, t_hbm, proj_hbm,
        orth_out, leaf_out, inner_out, upper_out, proj_out,
        gram, it_ref, own_up, orth_ref, leaf_ref, all_t, inner_ref, upper_ref, proj_ref, a, winv, uw, fetch_sem, store_sem):
    leaf = lax.axis_index("leaf")
    fetches = []
    for i, (x, y) in enumerate((
            (gram_hbm, gram), (t_hbm, all_t), (it_hbm.at[pl.ds(0, 7)], it_ref),
            (up_hbm.at[pl.ds(jnp.maximum(leaf - 1, 0), 1)], own_up),
            (orth_hbm, orth_ref), (leaf_hbm, leaf_ref), (proj_hbm, proj_ref))):
        fetches.append(pltpu.make_async_copy(x, y, fetch_sem.at[i]))
        fetches[-1].start()
    stores = []

    def store(src, dst):
        stores.append(pltpu.make_async_copy(src, dst, store_sem.at[len(stores)]))
        stores[-1].start()

    def pass_through():
        for i, (y, z) in enumerate(((orth_ref, orth_out), (leaf_ref, leaf_out), (proj_ref, proj_out))):
            fetches[4 + i].wait()
            store(y, z)
        fetches[1].wait()
        for b in range(4):
            at = 0
            for count in (8, 4, 2):
                for n in range(count):
                    inner_ref[4 * count - 1 + count * b + n] = all_t[b, at // 2, :, at % 2 * N:at % 2 * N + N]
                    at += 1
        store(inner_ref.at[pl.ds(7, 56)], inner_out.at[pl.ds(7, 56)])

    fetches[0].wait()
    factor_stack(gram, uw, a, winv, 16, eliminated=pass_through)
    for i in (2, 3):
        fetches[i].wait()

    def u(i):
        return uw[pl.ds(i * N, N), 0:N]

    def w(i):
        return uw[pl.ds(i * N, N), N:2 * N]

    inner_ref[0] = nt(nn(u(6), it_ref[0]), w(7))
    for n in range(2):
        inner_ref[1 + n] = nt(nn(u(4 + n), it_ref[1 + n]), w(6))
    for n in range(4):
        inner_ref[3 + n] = nt(nn(u(n), it_ref[3 + n]), w(4 + n // 2))
    store(inner_ref.at[pl.ds(0, 7)], inner_out.at[pl.ds(0, 7)])
    level = jnp.where(leaf % 2 == 1, 1, jnp.where(leaf % 4 == 2, 2, jnp.where(leaf % 8 == 4, 3, jnp.where(leaf % 16 == 8, 4, 5))))
    carried = nn(u(6 + level), own_up[0])
    renewed = nt(carried, w(jnp.minimum(7 + level, 11)))
    upper_ref[0] = jnp.where(leaf == 0, u(11), jnp.where(leaf == 16, carried, renewed))
    store(upper_ref, upper_out)
    for c in stores:
        c.wait()


def run_top(gram, it, up, orth, new_leaf, t, proj):
    hbm = pl.BlockSpec(memory_space=pl.ANY)
    sd = jax.ShapeDtypeStruct
    leaves = pltpu.VMEM((16, N, N), F32)
    one = pltpu.VMEM((1, N, N), F32)
    lanes = pltpu.VMEM((N, N, LANES), F32)
    return pl.pallas_call(
        top,
        out_shape=(sd((16, N, N), F32), sd((16, N, N), F32), sd((63, N, N), F32), sd((1, N, N), F32), sd((N, N, 256), F32)),
        in_specs=[hbm] * 7,
        out_specs=(hbm,) * 5,
        scratch_shapes=[
            pltpu.VMEM((16 * N, N), F32), pltpu.VMEM((7, N, N), F32), one, leaves, leaves,
            pltpu.VMEM((4, 7, N, 2 * N), F32), pltpu.VMEM((63, N, N), F32), one, pltpu.VMEM((N, N, 256), F32),
            lanes, lanes, pltpu.VMEM((16 * N, 2 * N), F32),
            pltpu.SemaphoreType.DMA((7,)), pltpu.SemaphoreType.DMA((6,)),
        ],
        compiler_params=pltpu.CompilerParams(vmem_limit_bytes=VMEM),
    )(gram, it, up, orth, new_leaf, t, proj)


def body(leaf_basis, leaf_transfer, inner_transfer, upper_transfer, coupling, pairs, counts):
    orth, new_leaf, all_t, gram, proj = run_tree(
        pairs, counts, leaf_basis, leaf_transfer, inner_transfer, upper_transfer, coupling)
    orth, new_leaf, inner, upper, proj = run_top(gram, inner_transfer, upper_transfer, orth, new_leaf, all_t, proj)
    return orth, new_leaf, inner, upper, jnp.transpose(proj, (2, 0, 1))


def solution(mesh):
    in_specs = (
        P(("leaf", "blk"), None, None),
        P(("leaf", "blk"), None, None),
        P("leaf", None, None),
        P(),
        P(("leaf", "blk"), None, None),
        P(("leaf", "blk"), None),
        P(("leaf", "blk")),
    )
    out_specs = (
        P(("leaf", "blk"), None, None),
        P(("leaf", "blk"), None, None),
        P("leaf", None, None),
        P("leaf", None, None),
        P(("leaf", "blk"), None, None),
    )
    return jax.shard_map(body, mesh=mesh, in_specs=in_specs, out_specs=out_specs, check_vma=False)
```

```python
import jax
import jax.numpy as jnp
from jax import lax
from jax.experimental import pallas as pl
from jax.experimental.pallas import tpu as pltpu
from jax.sharding import PartitionSpec as P

HIGH = lax.Precision.HIGHEST
F32 = jnp.float32
N = 64


def nn(a, b):
    return lax.dot_general(a, b, (((1,), (0,)), ((), ())), precision=HIGH, preferred_element_type=F32)


def tn(a, b):
    return lax.dot_general(a, b, (((0,), (0,)), ((), ())), precision=HIGH, preferred_element_type=F32)


def nt(a, b):
    return lax.dot_general(a, b, (((1,), (1,)), ((), ())), precision=HIGH, preferred_element_type=F32)


def sandwich(e, g):
    return tn(e, nn(g, e))


LANES = 128
COPIES = 29
VMEM = 60 * 2**20


def eliminate(a_ref, w_ref):
    sub = lax.broadcasted_iota(jnp.int32, (8, LANES), 0)

    def bc(x, i):
        return jnp.broadcast_to(x[i:i + 1, :], (8, LANES))

    def panel(p):
        k0 = 8 * p
        d = [a_ref[k0 + i, k0:k0 + 8, :] for i in range(8)]
        r, coef = [], {}
        for k in range(8):
            piv = bc(d[k], k)
            y = lax.rsqrt(piv)
            y = y * (1.5 - 0.5 * piv * y * y)
            r.append(y)
            d[k] = d[k] * y
            for i in range(k + 1, 8):
                coef[k, i] = bc(d[k], i)
                d[i] = d[i] - coef[k, i] * d[k]
        for i in range(8):
            a_ref[k0 + i, k0:k0 + 8, :] = d[i]

        def solve(x):
            for k in range(8):
                x[k] = x[k] * r[k]
                for i in range(k + 1, 8):
                    x[i] = x[i] - coef[k, i] * x[k]
            return x

        for jb in range(p + 1, 8):
            x = solve([a_ref[k0 + i, 8 * jb:8 * jb + 8, :] for i in range(8)])
            for i in range(8):
                a_ref[k0 + i, 8 * jb:8 * jb + 8, :] = x[i]
        for jb in range(p + 1):
            if jb < p:
                x = [w_ref[k0 + i, 8 * jb:8 * jb + 8, :] for i in range(8)]
            else:
                x = [jnp.where(sub == i, F32(1), F32(0)) for i in range(8)]
            x = solve(x)
            for i in range(8):
                w_ref[k0 + i, 8 * jb:8 * jb + 8, :] = x[i]

    def trail(p, row, targets):
        k0 = 8 * p
        for g in range(0, len(targets), 2):
            group = targets[g:g + 2]
            acc = {}
            for t, (ref, jb, fresh) in enumerate(group):
                for i in range(8):
                    acc[t, i] = jnp.zeros((8, LANES), F32) if fresh else ref[row + i, 8 * jb:8 * jb + 8, :]
            for k in range(8):
                pivots = [ref[k0 + k, 8 * jb:8 * jb + 8, :] for ref, jb, _ in group]
                for i in range(8):
                    c = jnp.broadcast_to(a_ref[k0 + k, pl.ds(row + i, 1), :], (8, LANES))
                    for t in range(len(group)):
                        acc[t, i] = acc[t, i] - c * pivots[t]
            for t, (ref, jb, _) in enumerate(group):
                for i in range(8):
                    ref[row + i, 8 * jb:8 * jb + 8, :] = acc[t, i]

    for p in range(8):
        panel(p)
        middle_block = (p + 9) // 2
        for start, stop in ((p + 1, middle_block), (middle_block, 8)):
            targets = [(a_ref, jb, False) for jb in range(start, 8)] + [(w_ref, jb, jb == p) for jb in range(p + 1)]

            def step(ib, _):
                trail(p, 8 * ib, targets)
                return 0
            lax.fori_loop(start, stop, step, 0)


def factor_stack(g_ref, uw_ref, a, w, n, loaded=None, eliminated=None):
    def load(k, _):
        a[k] = jnp.concatenate([g_ref[pl.ds(k, n, stride=N), :]] * (LANES // n), axis=0).T
        return 0
    lax.fori_loop(0, N, load, 0, unroll=8)
    if loaded is not None:
        loaded()
    eliminate(a, w)
    if eliminated is not None:
        eliminated()
    col = lax.broadcasted_iota(jnp.int32, (N, LANES), 0)

    def save(k, _):
        x = jnp.concatenate([jnp.where(col >= k, a[k], F32(0)), jnp.where(col <= k, w[k], F32(0))], axis=0)
        uw_ref[pl.ds(k, n, stride=N), :] = x.T[:n]
        return 0
    lax.fori_loop(0, N, save, 0, unroll=8)


BF = jnp.bfloat16


def split(x):
    h = x.astype(BF).astype(F32)
    return h, (x - h).astype(BF).astype(F32)


def cut(x):
    h, l = split(x)
    return h, l, pltpu.roll(h, N, 1), pltpu.roll(l, N, 1)


def halves():
    lane = lax.broadcasted_iota(jnp.int32, (16, 2 * N), 1)
    return jnp.where(lane < N, lane, lane - N)


def fold(x, y):
    col = halves()

    def ends(z):
        return jnp.where(col < 16, pltpu.roll(z[48:64], 80, 1), z[16:32])
    return jnp.concatenate(
        [x[0:16], ends(x), y[0:16], ends(y), jnp.where(col < 32, pltpu.roll(y[32:48], 96, 1), x[32:48])], axis=0)


def unfold(z):
    col = halves()
    zero = F32(0)

    def build(head, ends, third):
        return jnp.concatenate(
            [head, jnp.where(col < 16, zero, ends), third, pltpu.roll(jnp.where(col < 16, ends, zero), 48, 1)], axis=0)
    shared = z[64:80]
    return (build(z[0:16], z[16:32], jnp.where(col < 32, zero, shared)),
            build(z[32:48], z[48:64], pltpu.roll(jnp.where(col < 32, shared, zero), 32, 1)))


def tree(table_ref, count_ref, basis_hbm, lt_hbm, it_hbm, up_hbm, c_hbm, orth_out, newleaf_out, t_out, gram, out_ref,
         buf, s, r, cols, rows, basis_ref, lt_ref, e, tmp, orth_ref, newleaf_ref, gram_low, uw_low, pack_ref, tpack_ref, it_ref, near_up, far_up, all_u, all_t, quad, octet, four, a, winv,
           send_sem, recv_sem, fetch_sem, store_sem, own_sem):
    leaf, blk = lax.axis_index("leaf"), lax.axis_index("blk")
    low, high = leaf % 8, leaf // 8
    zup, zdown, zfar = [{"leaf": leaf, "blk": (blk + i) % 4} for i in (1, 3, 2)]
    right = {"leaf": (leaf + 1) % 32, "blk": blk}
    left = {"leaf": (leaf + 31) % 32, "blk": blk}
    mid = [{"leaf": high * 8 + (low + i) % 8, "blk": blk} for i in range(1, 8)]
    far = [{"leaf": (high + i) % 4 * 8 + low, "blk": blk} for i in range(1, 4)]
    peers = [zup, zdown, zfar, right, left] + mid + far
    barrier = pltpu.get_barrier_semaphore()
    for peer in peers:
        pl.semaphore_signal(barrier, inc=1, device_id=peer, device_id_type=pl.DeviceIdType.MESH)
    fetches = {}
    wanted = [("basis", basis_hbm, basis_ref), ("lt", lt_hbm, lt_ref)]
    for count, at in ((8, 0), (4, 8), (2, 12), (1, 14)):
        wanted.append(("e%d" % count, it_hbm.at[pl.ds(4 * count - 1 + count * blk, count)], e.at[pl.ds(at, count)]))
    wanted += [
        ("it", it_hbm.at[pl.ds(0, 3)], it_ref),
        ("near", up_hbm.at[pl.ds(high * 8, 7)], near_up), ("far0", up_hbm.at[pl.ds(7, 1)], far_up.at[pl.ds(0, 1)]),
        ("far1", up_hbm.at[pl.ds(23, 1)], far_up.at[pl.ds(1, 1)]), ("c", c_hbm, buf)]
    for i, (name, x, y) in enumerate(wanted):
        fetches[name] = pltpu.make_async_copy(x, y, fetch_sem.at[i])
        fetches[name].start()
    used, stores = [], []

    def push(src, dst, peer):
        i = len(used)
        c = pltpu.make_async_remote_copy(
            src_ref=src, dst_ref=dst, send_sem=send_sem.at[i], recv_sem=recv_sem.at[i],
            device_id=peer, device_id_type=pl.DeviceIdType.MESH)
        c.start()
        used.append(c)
        return c

    def store(src, dst):
        c = pltpu.make_async_copy(src, dst, store_sem.at[len(stores)])
        c.start()
        stores.append(c)

    def block(d, b, start=0, count=4):
        return all_u.at[pl.ds((d * 4 + b) * 4 + start, count)]

    def keep(i, g):
        gram[i * N:i * N + N, :] = g

    fetches["basis"].wait()
    fetches["lt"].wait()
    for c in range(16):
        b = basis_ref[c]
        g = tn(b, b)
        gram_low[c * N:c * N + N, :] = g
        tmp[c] = sandwich(lt_ref[c], g)
    at, done = 16, 0
    for count in (8, 4, 2, 1):
        fetches["e%d" % count].wait()
        for n in range(count):
            g = tmp[done + 2 * n] + tmp[done + 2 * n + 1]
            gram_low[(at + n) * N:(at + n) * N + N, :] = g
            m = sandwich(e[at - 16 + n], g)
            if count == 1:
                quad[blk] = jnp.concatenate([g, m], axis=1)
                gram_low[31 * N:32 * N, :] = g
            else:
                tmp[done + 2 * count + n] = m
        done += 2 * count
        at += count
    pl.semaphore_wait(barrier, len(peers))
    quads = [push(quad.at[blk], quad.at[blk], peer) for peer in (zup, zdown, zfar)]
    octets = []

    def subtree_top():
        fetches["it"].wait()
        for c in quads:
            c.wait_recv()
        root = None
        for n in range(2):
            keep(2 * n, quad[2 * n, :, 0:N])
            keep(2 * n + 1, quad[2 * n + 1, :, 0:N])
            g = quad[2 * n, :, N:2 * N] + quad[2 * n + 1, :, N:2 * N]
            keep(4 + n, g)
            m = sandwich(it_ref[1 + n], g)
            root = m if root is None else root + m
        keep(6, root)
        octet[low] = sandwich(it_ref[0], root)
        octets.extend([push(octet.at[low], octet.at[low], peer) for peer in mid])

    factor_stack(gram_low, uw_low, a, winv, 32, eliminated=subtree_top)

    def u_low(i):
        return uw_low[i * N:i * N + N, 0:N]

    def w_low(i):
        return uw_low[i * N:i * N + N, N:2 * N]

    for c in range(4):
        pack_ref[c] = fold(jnp.concatenate([u_low(4 * c), u_low(4 * c + 1)], axis=1),
                           jnp.concatenate([u_low(4 * c + 2), u_low(4 * c + 3)], axis=1))
    own_u = pltpu.make_async_copy(pack_ref, block(1, blk), own_sem.at[0])
    own_u.start()
    u_up = push(pack_ref, block(1, blk), zup)
    u_down = push(pack_ref, block(1, blk), zdown)
    sides = [(push(pack_ref, block(0, blk), right), 0, blk), (push(pack_ref, block(2, blk), left), 2, blk)]
    for c in range(16):
        orth_ref[c] = nt(basis_ref[c], w_low(c))
    store(orth_ref, orth_out)
    for c in range(8):
        x = jnp.concatenate([nn(u_low(2 * c), lt_ref[2 * c]), nn(u_low(2 * c + 1), lt_ref[2 * c + 1])], axis=0)
        x = nt(x, w_low(16 + c))
        newleaf_ref[2 * c] = x[:N]
        newleaf_ref[2 * c + 1] = x[N:]
    store(newleaf_ref, newleaf_out)

    lane = lax.broadcasted_iota(jnp.int32, (N, 2 * N), 1)
    lower_lanes = lane < N

    def turn(k, _):
        x = jnp.concatenate([buf[k, :, 0:128], buf[k, :, 128:256]], axis=0)
        s[pl.ds(k, 128, stride=N), :] = x.T
        return 0
    fetches["c"].wait()
    lax.fori_loop(0, N, turn, 0, unroll=8)

    at, pair = 16, 0
    for count in (8, 4, 2):
        for n in range(0, count, 2):
            x = jnp.concatenate([nn(u_low(at + n), e[at + n - 16]), nn(u_low(at + n + 1), e[at + n - 15])], axis=0)
            x = nt(x, w_low(at + count + n // 2))
            tpack_ref[pair] = jnp.concatenate([x[:N], x[N:]], axis=1)
            pair += 1
        at += count
    store(tpack_ref, t_out.at[blk])

    below, above, beyond = (blk + 3) % 4, (blk + 1) % 4, (blk + 2) % 4

    def forward(b):
        sides.extend([(push(block(1, b), block(0, b), right), 0, b), (push(block(1, b), block(2, b), left), 2, b)])

    def prepare(q, _):
        for t, x in enumerate(unfold(all_u[q])):
            h, l, hr, lr = cut(x)
            at = 4 * q + 2 * t
            cols[at] = jnp.concatenate([jnp.where(lower_lanes, h, hr), jnp.where(lower_lanes, l, lr)], axis=1).astype(BF)
            cols[at + 1] = jnp.concatenate([jnp.where(lower_lanes, hr, h), jnp.where(lower_lanes, lr, l)], axis=1).astype(BF)
        return 0

    def prepare_rows(q, _):
        for t, x in enumerate(unfold(all_u[16 + q])):
            h, l, hr, lr = cut(x)
            rows[4 * q + 2 * t] = jnp.where(lower_lanes, h, lr).astype(BF)
            rows[4 * q + 2 * t + 1] = jnp.where(lower_lanes, hr, l).astype(BF)
        return 0

    def split_block(d, b):
        first = (d * 4 + b) * 4
        if d == 1:
            lax.fori_loop(0, 4, lambda q, _: prepare_rows(b * 4 + q, _), 0, unroll=4)
        lax.fori_loop(0, 4, lambda q, _: prepare(first + q, _), 0, unroll=4)

    u_up.wait_recv()
    half_up = push(block(1, below, 0, 2), block(1, below, 0, 2), zup)
    u_down.wait_recv()
    half_down = push(block(1, above, 2, 2), block(1, above, 2, 2), zdown)
    forward(below)
    forward(above)
    t_up = push(tpack_ref, all_t.at[blk], zup)
    t_down = push(tpack_ref, all_t.at[blk], zdown)
    own_u.wait()
    for b in (blk, below, above):
        split_block(1, b)

    half_up.wait_recv()
    half_down.wait_recv()
    forward(beyond)
    split_block(1, beyond)
    for name in ("near", "far0", "far1"):
        fetches[name].wait()
    for c in octets:
        c.wait_recv()
    first = [octet[2 * n] + octet[2 * n + 1] for n in range(4)]
    keep(7, octet[low // 2 * 2] + octet[low // 2 * 2 + 1])
    images = [sandwich(near_up[2 * n], first[n]) for n in range(4)]
    second = [images[2 * n] + images[2 * n + 1] for n in range(2)]
    keep(8, jnp.where(low < 4, second[0], second[1]))
    images = [sandwich(near_up[4 * n + 1], second[n]) for n in range(2)]
    third = images[0] + images[1]
    keep(9, third)
    four[high] = sandwich(near_up[3], third)
    fours = [push(four.at[high], four.at[high], peer) for peer in far]

    t_up.wait_recv()
    t_half_up = push(all_t.at[below, pl.ds(0, 4)], all_t.at[below, pl.ds(0, 4)], zup)
    t_down.wait_recv()
    t_half_down = push(all_t.at[above, pl.ds(4, 3)], all_t.at[above, pl.ds(4, 3)], zdown)
    for b in (below, above):
        store(all_t.at[b], t_out.at[b])
    for c, d, b in sides:
        c.wait_recv()
        split_block(d, b)

    base = leaf * 64

    def slot(k, d):
        i = jnp.clip(table_ref[0, k] - base, 0, 63)
        j = jnp.clip(table_ref[1, k] - base + 64, 0, 191)
        d = d.astype(BF)
        y = lax.dot_general(jnp.concatenate([d, d], axis=1), cols[j], (((1,), (1,)), ((), ())), preferred_element_type=F32)
        h = y.astype(BF)
        l = (y - h.astype(F32)).astype(BF)
        x = rows[i]
        return lax.dot_general(jnp.concatenate([x, x], axis=1), jnp.concatenate([h, h, l, l], axis=0),
                               (((1,), (0,)), ((), ())), preferred_element_type=F32)

    def both(k, _):
        at = pl.ds(pl.multiple_of(k * N, N), N)
        h, l, hr, lr = cut(s[at, :])
        r[at, :] = jnp.concatenate([slot(k, jnp.where(lower_lanes, h, lr)), slot(k + 128, jnp.where(lower_lanes, hr, l))], axis=1)
        return 0
    lax.fori_loop(0, 128, both, 0, unroll=32)

    for c in fours:
        c.wait_recv()
    fourth = [four[2 * n] + four[2 * n + 1] for n in range(2)]
    keep(10, jnp.where(high < 2, fourth[0], fourth[1]))
    images = [sandwich(far_up[n], fourth[n]) for n in range(2)]
    for n in range(11, 16):
        keep(n, images[0] + images[1])

    live = count_ref[0]

    def back(k, _):
        x = r[pl.ds(k, 128, stride=N), :].T
        buf[k, :, 0:128] = jnp.where(lane < live, x[:N], F32(0))
        buf[k, :, 128:256] = jnp.where(lane + 128 < live, x[N:], F32(0))
        return 0
    for q in range(4):
        lax.fori_loop(16 * q, 16 * q + 16, back, 0, unroll=8)
        part = pl.ds(16 * q, 16)
        store(buf.at[part], out_ref.at[part])

    t_half_up.wait_recv()
    t_half_down.wait_recv()
    store(all_t.at[beyond], t_out.at[beyond])
    for c in used:
        c.wait_send()
    for c in stores:
        c.wait()


def run_tree(pairs, counts, basis, lt, it, up, coupling):
    vm = pl.BlockSpec(memory_space=pltpu.VMEM)
    sm = pl.BlockSpec(memory_space=pltpu.SMEM)
    hbm = pl.BlockSpec(memory_space=pl.ANY)
    sd = jax.ShapeDtypeStruct
    leaves = pltpu.VMEM((16, N, N), F32)
    lanes = pltpu.VMEM((N, N, LANES), F32)
    return pl.pallas_call(
        tree,
        out_shape=(sd((16, N, N), F32), sd((16, N, N), F32), sd((4, 7, N, 2 * N), F32), sd((16 * N, N), F32), sd((N, N, 256), F32)),
        in_specs=[sm, sm] + [hbm] * 5,
        out_specs=(hbm, hbm, hbm, vm, hbm),
        scratch_shapes=[
            pltpu.VMEM((N, N, 256), F32), pltpu.VMEM((128 * N, 2 * N), F32), pltpu.VMEM((128 * N, 2 * N), F32),
            pltpu.VMEM((192, N, 4 * N), BF), pltpu.VMEM((64, N, 2 * N), BF),
            leaves, leaves, pltpu.VMEM((15, N, N), F32), pltpu.VMEM((32, N, N), F32), leaves, leaves,
            pltpu.VMEM((32 * N, N), F32), pltpu.VMEM((32 * N, 2 * N), F32),
            pltpu.VMEM((4, 80, 2 * N), F32), pltpu.VMEM((7, N, 2 * N), F32), pltpu.VMEM((3, N, N), F32),
            pltpu.VMEM((7, N, N), F32), pltpu.VMEM((2, N, N), F32),
            pltpu.VMEM((48, 80, 2 * N), F32), pltpu.VMEM((4, 7, N, 2 * N), F32),
            pltpu.VMEM((4, N, 2 * N), F32), pltpu.VMEM((8, N, N), F32), pltpu.VMEM((4, N, N), F32), lanes, lanes,
            pltpu.SemaphoreType.DMA((COPIES,)), pltpu.SemaphoreType.DMA((COPIES,)), pltpu.SemaphoreType.DMA((11,)),
            pltpu.SemaphoreType.DMA((10,)), pltpu.SemaphoreType.DMA((1,)),
        ],
        compiler_params=pltpu.CompilerParams(collective_id=0, has_side_effects=True, vmem_limit_bytes=VMEM),
    )(pairs.T, counts, basis, lt, it, up, jnp.transpose(coupling, (1, 2, 0)))


def top(gram_hbm, it_hbm, up_hbm, orth_hbm, leaf_hbm, t_hbm, proj_hbm,
        orth_out, leaf_out, inner_out, upper_out, proj_out,
        gram, it_ref, own_up, orth_ref, leaf_ref, all_t, inner_ref, upper_ref, proj_ref, a, winv, uw, fetch_sem, store_sem):
    leaf = lax.axis_index("leaf")
    fetches = []
    for i, (x, y) in enumerate((
            (gram_hbm, gram), (t_hbm, all_t), (it_hbm.at[pl.ds(0, 7)], it_ref),
            (up_hbm.at[pl.ds(jnp.maximum(leaf - 1, 0), 1)], own_up),
            (orth_hbm, orth_ref), (leaf_hbm, leaf_ref), (proj_hbm, proj_ref))):
        fetches.append(pltpu.make_async_copy(x, y, fetch_sem.at[i]))
        fetches[-1].start()
    stores = []

    def store(src, dst):
        stores.append(pltpu.make_async_copy(src, dst, store_sem.at[len(stores)]))
        stores[-1].start()

    def pass_through():
        for i, (y, z) in enumerate(((orth_ref, orth_out), (leaf_ref, leaf_out), (proj_ref, proj_out))):
            fetches[4 + i].wait()
            store(y, z)
        fetches[1].wait()
        for b in range(4):
            at = 0
            for count in (8, 4, 2):
                for n in range(count):
                    inner_ref[4 * count - 1 + count * b + n] = all_t[b, at // 2, :, at % 2 * N:at % 2 * N + N]
                    at += 1
        store(inner_ref.at[pl.ds(7, 56)], inner_out.at[pl.ds(7, 56)])

    fetches[0].wait()
    factor_stack(gram, uw, a, winv, 16, eliminated=pass_through)
    for i in (2, 3):
        fetches[i].wait()

    def u(i):
        return uw[pl.ds(i * N, N), 0:N]

    def w(i):
        return uw[pl.ds(i * N, N), N:2 * N]

    inner_ref[0] = nt(nn(u(6), it_ref[0]), w(7))
    for n in range(2):
        inner_ref[1 + n] = nt(nn(u(4 + n), it_ref[1 + n]), w(6))
    for n in range(4):
        inner_ref[3 + n] = nt(nn(u(n), it_ref[3 + n]), w(4 + n // 2))
    store(inner_ref.at[pl.ds(0, 7)], inner_out.at[pl.ds(0, 7)])
    level = jnp.where(leaf % 2 == 1, 1, jnp.where(leaf % 4 == 2, 2, jnp.where(leaf % 8 == 4, 3, jnp.where(leaf % 16 == 8, 4, 5))))
    carried = nn(u(6 + level), own_up[0])
    renewed = nt(carried, w(jnp.minimum(7 + level, 11)))
    upper_ref[0] = jnp.where(leaf == 0, u(11), jnp.where(leaf == 16, carried, renewed))
    store(upper_ref, upper_out)
    for c in stores:
        c.wait()


def run_top(gram, it, up, orth, new_leaf, t, proj):
    hbm = pl.BlockSpec(memory_space=pl.ANY)
    sd = jax.ShapeDtypeStruct
    leaves = pltpu.VMEM((16, N, N), F32)
    one = pltpu.VMEM((1, N, N), F32)
    lanes = pltpu.VMEM((N, N, LANES), F32)
    return pl.pallas_call(
        top,
        out_shape=(sd((16, N, N), F32), sd((16, N, N), F32), sd((63, N, N), F32), sd((1, N, N), F32), sd((N, N, 256), F32)),
        in_specs=[hbm] * 7,
        out_specs=(hbm,) * 5,
        scratch_shapes=[
            pltpu.VMEM((16 * N, N), F32), pltpu.VMEM((7, N, N), F32), one, leaves, leaves,
            pltpu.VMEM((4, 7, N, 2 * N), F32), pltpu.VMEM((63, N, N), F32), one, pltpu.VMEM((N, N, 256), F32),
            lanes, lanes, pltpu.VMEM((16 * N, 2 * N), F32),
            pltpu.SemaphoreType.DMA((7,)), pltpu.SemaphoreType.DMA((6,)),
        ],
        compiler_params=pltpu.CompilerParams(vmem_limit_bytes=VMEM),
    )(gram, it, up, orth, new_leaf, t, proj)


def body(leaf_basis, leaf_transfer, inner_transfer, upper_transfer, coupling, pairs, counts):
    orth, new_leaf, all_t, gram, proj = run_tree(
        pairs, counts, leaf_basis, leaf_transfer, inner_transfer, upper_transfer, coupling)
    orth, new_leaf, inner, upper, proj = run_top(gram, inner_transfer, upper_transfer, orth, new_leaf, all_t, proj)
    return orth, new_leaf, inner, upper, jnp.transpose(proj, (2, 0, 1))


def solution(mesh):
    in_specs = (
        P(("leaf", "blk"), None, None),
        P(("leaf", "blk"), None, None),
        P("leaf", None, None),
        P(),
        P(("leaf", "blk"), None, None),
        P(("leaf", "blk"), None),
        P(("leaf", "blk")),
    )
    out_specs = (
        P(("leaf", "blk"), None, None),
        P(("leaf", "blk"), None, None),
        P("leaf", None, None),
        P("leaf", None, None),
        P(("leaf", "blk"), None, None),
    )
    return jax.shard_map(body, mesh=mesh, in_specs=in_specs, out_specs=out_specs, check_vma=False)
```
